32 devices in a mesh: tile: 8 (over z, x), dp: 4 (over y, core).
Axes of the slice: x: 2, y: 2, z: 4, core: 2. Of those that a mesh axis runs over, the one named last changes fastest.
Arguments:
- features: bfloat16 [512, 256, 128], P('tile'), may hold values from -6 to 6
- target_field: bfloat16 [512, 256], P('tile'), may hold values from -3 to 3
- owner_tile: int32 [128, 1], P(('tile', 'dp')), may hold values from 0 to 7; in each aligned block of 4 rows (0 to 3, 4 to 7, ...) at most 2 rows name the same one
- row_offset: int32 [128], P(('tile', 'dp')), may hold values from 0 to 48
- column_start: int32 [128], P(('tile', 'dp')), may hold values from 0 to 240
- noise_level: int32 [128], P(('tile', 'dp')), may hold values from 0 to 31
- icing_count: int32 [128], P(('tile', 'dp')), may hold values from 1 to 4
- noise_draw: float32 [128, 16, 16], P(('tile', 'dp')), may hold values from -6 to 6
- w_a: bfloat16 [1152, 512], replicated, may hold values from -0.1875 to 0.1875
- w_u: float32 [9, 512], replicated, may hold values from -2 to 2
- b_a: float32 [512], replicated, may hold values from -3 to 3
- e_a: float32 [512], replicated, may hold values from -6 to 6
- w_b: bfloat16 [4608, 128], replicated, may hold values from -0.09375 to 0.09375
- b_b: float32 [128], replicated, may hold values from -3 to 3
- w_o: float32 [128], replicated, may hold values from -0.5 to 0.5
Outputs:
- losses: float32 [128], P(('tile', 'dp'))
- upd_a: float32 [512, 1152], P(('tile', 'dp'))
- upd_b: float32 [512, 1152], P(('tile', 'dp'))
The draws below stay inside these ranges and needn't reach their ends.
Inputs may be any that keep to these rules, and one draw needn't show every extreme that they name: `owner_tile`: among the 4 patches of one device no tile is named more than 2 times, a bound that some block reaches. `row_offset`: a patch's rows lie inside its tile.
All inputs are finite; a program needn't handle non-finite values.
Results may differ from the reference program's by a relative error of at most 0.0027.
Values may be sent and summed in bfloat16 or wider, within the bound.
No kernel may reach another device: no remote copies, remote signals or barrier semaphores. Data moves between devices by JAX's collectives and lax.ppermute only.
A program may use at most 128 MiB of HBM per device.

```python
import math
import jax
import jax.numpy as jnp
import numpy as np
from jax import lax

C = 128
HID = 512
P_SIZE = 16
LEVELS = 32
PATCH_DEV = 4
TILE_ROWS = 64
W = 256
CAP = 2
GRID_ROWS = 512
PATCHES = 128
N_TILE = 8


def place_ends(array, key, low, high):
    shape = array.shape
    spot = [jax.random.randint(jax.random.fold_in(key, axis), (), 0, shape[axis]) for axis in range(len(shape))]
    array = array.at[tuple(spot)].set(low)
    longest = shape.index(max(shape))
    spot[longest] = (spot[longest] + 1) % shape[longest]
    return array.at[tuple(spot)].set(high)


def levels(stream_key, dims, cuts, least, largest):
    gain, own = 1.0, jax.random.fold_in(stream_key, 6)
    for axis_at, shards_of in cuts:
        draws = jnp.exp(jax.random.uniform(jax.random.fold_in(own, axis_at), (shards_of,), jnp.float32, least / len(cuts), largest / len(cuts)))
        gain = gain * jnp.repeat(draws, dims[axis_at] // shards_of).reshape([-1 if axis == axis_at else 1 for axis in range(len(dims))])
    return gain


def routed_block(own_key, own, number, rows, amount, top, reach, skew):
    order = jax.random.permutation(own_key, amount)
    packed, common = load_shares(amount, rows * top, reach, skew, True), load_shares(amount, rows * top, reach, skew, False)
    places = jnp.arange(amount)

    def named(lengths, turn):
        used = int((lengths > 0).sum())
        fixed = max(1, used // 4)
        passed = fixed + (places - fixed + turn * (used - fixed)) % max(1, amount - fixed)
        return jnp.zeros((amount,), jnp.int32).at[order[jnp.where(places < fixed, places, passed)]].set(jnp.asarray(lengths, jnp.int32))

    lengths = jnp.where(number % 4 == 0, named(packed, number // 4), named(common, number - number // 4 - 1))
    mixed = jax.random.permutation(jax.random.fold_in(own, 3), amount)
    source_of, taker = mixed[0:amount // 2 * 2:2], mixed[1:amount // 2 * 2:2]
    slack = jnp.minimum(lengths[source_of] - 1, reach - lengths[taker]) // 2
    slack = jnp.where((source_of == order[0]) | (taker == order[0]) | (lengths[taker] == 0), 0, jnp.maximum(slack, 0))
    passed = jax.random.randint(jax.random.fold_in(own, 4), (amount // 2,), 0, 1 << 20) % (slack + 1)
    lengths = lengths.at[source_of].add(-passed).at[taker].add(passed)
    labels = jnp.searchsorted(jnp.cumsum(lengths), jnp.arange(rows * top), side="right").astype(jnp.int32)
    grid = labels.reshape(top, rows).T
    grid = grid[jax.random.permutation(jax.random.fold_in(own, 1), rows)]
    turn = jax.random.randint(jax.random.fold_in(own, 2), (rows, 1), 0, top)
    return jnp.take_along_axis(grid, (jnp.arange(top)[None, :] + turn) % top, axis=1)


def load_shares(amount, total, reach, skew, full):
    weights = [(1 << 20) // math.isqrt(grade ** skew) + 1 for grade in range(1, amount + 1)]
    largest = reach if full else min(reach, max(-(-total // amount), total * weights[0] // sum(weights)))
    least = 1 if total - largest >= amount - 1 else 0
    given, spare = [largest] + [least] * (amount - 1), total - largest - least * (amount - 1)
    while spare > 0:
        movable = [i for i in range(1, amount) if given[i] < largest] or [i for i in range(1, amount) if given[i] < reach]
        mass, budget = sum([weights[i] for i in movable]), spare
        for i in movable:
            addition = min(reach - given[i], max(1, budget * weights[i] // mass), spare)
            given[i] = given[i] + addition
            spare = spare - addition
    return np.array(given)


def scatter_about(own_key, extent, scale, limit, cuts=(), kind=jnp.bfloat16):
    level = levels(own_key, extent, cuts, -0.22, 0.18) if cuts else 1.0
    drawn = jax.random.normal(own_key, extent, jnp.float32) * scale * level
    return jnp.minimum(jnp.maximum(drawn, -limit), limit).astype(kind)


def setup_inputs(seed: int = 0) -> dict:
    keys = jax.random.split(jax.random.key(seed), 16)
    features = scatter_about(keys[0], (GRID_ROWS, W, C), 1.0, 6.0, ((0, 8),))
    target_field = scatter_about(keys[1], (GRID_ROWS, W), 0.5, 3.0, ((0, 8),))
    owner_tile_keys = jax.random.split(jax.random.fold_in(keys[2], 1), PATCHES // PATCH_DEV)
    owner_tile_turns = jax.random.permutation(jax.random.fold_in(keys[2], 3), PATCHES // PATCH_DEV)
    owner_tile = jax.vmap(lambda own, number: routed_block(jax.random.fold_in(keys[2], 2), own, number, PATCH_DEV, N_TILE, 1, CAP, 2))(owner_tile_keys, owner_tile_turns).reshape((PATCHES, 1))
    row_offset = place_ends(jax.random.randint(keys[3], (PATCHES,), 0, TILE_ROWS - P_SIZE + 1), jax.random.fold_in(keys[3], 1), 0, TILE_ROWS - P_SIZE).astype(jnp.int32)
    column_start = place_ends(jax.random.randint(keys[4], (PATCHES,), 0, W - P_SIZE + 1), jax.random.fold_in(keys[4], 1), 0, W - P_SIZE).astype(jnp.int32)
    noise_level = place_ends(jax.random.randint(keys[5], (PATCHES,), 0, LEVELS), jax.random.fold_in(keys[5], 1), 0, LEVELS - 1).astype(jnp.int32)
    icing_count = place_ends(jax.random.randint(keys[6], (PATCHES,), 1, 5), jax.random.fold_in(keys[6], 1), 1, 4).astype(jnp.int32)
    noise_draw = scatter_about(keys[7], (PATCHES, P_SIZE, P_SIZE), 1.0, 6.0, ((0, 32),), jnp.float32)
    w_a = scatter_about(keys[8], (9 * C, HID), (9 * C) ** -0.5, 0.1875)
    w_u = scatter_about(keys[9], (9, HID), 9 ** -0.5, 2.0, (), jnp.float32)
    b_a = scatter_about(keys[10], (HID,), 0.5, 3.0, (), jnp.float32)
    e_a = scatter_about(keys[11], (HID,), 1.0, 6.0, (), jnp.float32)
    w_b = scatter_about(keys[12], (9 * HID, C), (9 * HID) ** -0.5, 0.09375)
    b_b = scatter_about(keys[13], (C,), 0.5, 3.0, (), jnp.float32)
    w_o = scatter_about(keys[14], (C,), C ** -0.5, 0.5, (), jnp.float32)
    return {"features": features, "target_field": target_field, "owner_tile": owner_tile, "row_offset": row_offset, "column_start": column_start, "noise_level": noise_level, "icing_count": icing_count, "noise_draw": noise_draw, "w_a": w_a, "w_u": w_u, "b_a": b_a, "e_a": e_a, "w_b": w_b, "b_b": b_b, "w_o": w_o}


SIGMA_LOW = 0.02
SIGMA_HIGH = 80.0
SIGMA_DATA = 0.5
EPSILON = 1e-06

def silu_prime(values):
    sigmoid_val = jax.nn.sigmoid(values)
    return sigmoid_val * (1.0 + values * (1.0 - sigmoid_val))

def tap_window(padded, shift_row, shift_col, side_len):
    window = padded[:, shift_row:shift_row + side_len, shift_col:shift_col + side_len]
    return window.reshape((-1,) + padded.shape[3:])

def patch_terms(patch_feats, patch_target, noise_draw, noise_level, icing_count, w_a, w_u, b_a, e_a, w_b, b_b, w_o):
    npatch = patch_feats.shape[0]
    side_len = patch_feats.shape[1]
    channels = patch_feats.shape[3]
    hidden_width = w_a.shape[1]
    pixels = side_len * side_len
    log_step = (math.log(SIGMA_HIGH) - math.log(SIGMA_LOW)) / (LEVELS - 1)
    sigmas = jnp.exp(math.log(SIGMA_LOW) + noise_level.astype(jnp.float32) * log_step)
    variance = sigmas * sigmas + SIGMA_DATA * SIGMA_DATA
    scale_in = 1.0 / jnp.sqrt(variance)
    scale_skip = SIGMA_DATA * SIGMA_DATA / variance
    scale_out = sigmas * SIGMA_DATA * scale_in
    noise_embed = jnp.log(sigmas) / 4.0
    clean_field = patch_target.astype(jnp.float32)
    noisy_field = clean_field + sigmas[:, None, None] * noise_draw
    aim_value = ((clean_field - scale_skip[:, None, None] * noisy_field) / scale_out[:, None, None]).reshape(-1)
    scaled_in = jnp.pad(scale_in[:, None, None] * noisy_field, ((0, 0), (1, 1), (1, 1)))
    feat_pad = jnp.pad(patch_feats, ((0, 0), (1, 1), (1, 1), (0, 0)))
    embed_rows = jnp.repeat(noise_embed, pixels)
    pre_a = b_a[None, :] + embed_rows[:, None] * e_a[None, :]
    for tap_index in range(9):
        shift_row, shift_col = (tap_index // 3, tap_index % 3)
        window = tap_window(feat_pad, shift_row, shift_col, side_len)
        pre_a = pre_a + jnp.dot(window, w_a[tap_index * channels:(tap_index + 1) * channels], preferred_element_type=jnp.float32)
        pre_a = pre_a + tap_window(scaled_in, shift_row, shift_col, side_len)[:, None] * w_u[tap_index][None, :]
    hidden_act = jax.nn.silu(pre_a).astype(jnp.bfloat16)
    act_pad = jnp.pad(hidden_act.reshape(npatch, side_len, side_len, hidden_width), ((0, 0), (1, 1), (1, 1), (0, 0)))
    pre_b = jnp.zeros((npatch * pixels, channels), jnp.float32) + b_b[None, :]
    for tap_index in range(9):
        shift_row, shift_col = (tap_index // 3, tap_index % 3)
        window = tap_window(act_pad, shift_row, shift_col, side_len)
        pre_b = pre_b + jnp.dot(window, w_b[tap_index * hidden_width:(tap_index + 1) * hidden_width], preferred_element_type=jnp.float32)
    out_act = jax.nn.silu(pre_b)
    output_map = jnp.dot(out_act, w_o, precision=lax.Precision.HIGHEST)
    residual = output_map - aim_value
    weights = jnp.repeat(icing_count.astype(jnp.float32), pixels)
    losses = lax.optimization_barrier(jnp.mean((weights * residual * residual).reshape(npatch, pixels), axis=1))
    grad_final = 2.0 * weights * residual / pixels
    grad_pre_b = (grad_final[:, None] * w_o[None, :] * silu_prime(pre_b)).astype(jnp.bfloat16)
    grad_hidden = jnp.zeros((npatch, side_len + 2, side_len + 2, hidden_width), jnp.float32)
    parts_b = []
    for tap_index in range(9):
        shift_row, shift_col = (tap_index // 3, tap_index % 3)
        window = tap_window(act_pad, shift_row, shift_col, side_len)
        parts_b.append(lax.dot_general(window, grad_pre_b, (((0,), (0,)), ((), ())), preferred_element_type=jnp.float32))
        back_term = lax.dot_general(grad_pre_b, w_b[tap_index * hidden_width:(tap_index + 1) * hidden_width], (((1,), (1,)), ((), ())), preferred_element_type=jnp.float32)
        grad_hidden = grad_hidden.at[:, shift_row:shift_row + side_len, shift_col:shift_col + side_len].add(back_term.reshape(npatch, side_len, side_len, hidden_width))
    grad_pre_a = (grad_hidden[:, 1:-1, 1:-1].reshape(-1, hidden_width) * silu_prime(pre_a)).astype(jnp.bfloat16)
    parts_a = []
    for tap_index in range(9):
        shift_row, shift_col = (tap_index // 3, tap_index % 3)
        window = tap_window(feat_pad, shift_row, shift_col, side_len)
        parts_a.append(lax.dot_general(grad_pre_a, window, (((0,), (0,)), ((), ())), preferred_element_type=jnp.float32))
    return (losses, jnp.concatenate(parts_a, axis=1), jnp.concatenate(parts_b, axis=1))

def reference(features, target_field, owner_tile, row_offset, column_start, noise_level, icing_count, noise_draw, w_a, w_u, b_a, e_a, w_b, b_b, w_o):
    total_patches = owner_tile.shape[0]
    group_size = min(total_patches, PATCH_DEV * 8)
    groups = total_patches // group_size
    grid_row = (owner_tile[:, 0] * TILE_ROWS + row_offset).astype(jnp.int32)

    def extract(source_row, source_col):
        anchor = jnp.zeros((), jnp.int32)
        feat_block = lax.dynamic_slice(features, (source_row, source_col, anchor), (P_SIZE, P_SIZE, C))
        target_block = lax.dynamic_slice(target_field, (source_row, source_col), (P_SIZE, P_SIZE))
        return (feat_block, target_block)

    def one_group(totals, inputs):
        rows_in, cols_in, levels_in, counts_in, noise_in = inputs
        blocks, fields = jax.vmap(extract)(rows_in, cols_in)
        group_losses, part_a, part_b = patch_terms(blocks, fields, noise_in, levels_in, counts_in, w_a, w_u, b_a, e_a, w_b, b_b, w_o)
        return ((totals[0] + part_a, totals[1] + part_b), group_losses)
    inputs = (grid_row.reshape(groups, group_size), column_start.astype(jnp.int32).reshape(groups, group_size), noise_level.reshape(groups, group_size), icing_count.reshape(groups, group_size), noise_draw.reshape(groups, group_size, P_SIZE, P_SIZE))
    start_sum = (jnp.zeros((HID, 9 * C), jnp.float32), jnp.zeros((HID, 9 * C), jnp.float32))
    (grad_a, grad_b), losses = lax.scan(one_group, start_sum, inputs)
    upd_a = grad_a / jnp.sqrt(jnp.mean(grad_a * grad_a) + EPSILON)
    upd_b = grad_b / jnp.sqrt(jnp.mean(grad_b * grad_b) + EPSILON)
    return (losses.reshape(-1), upd_a, upd_b)
```

```python
import functools
import math

import jax
import jax.numpy as jnp
from jax import lax
from jax.experimental import pallas as pl
from jax.experimental.pallas import tpu as pltpu
from jax.sharding import PartitionSpec as P

C = 128
HID = 512
P_SIZE = 16
LEVELS = 32
CELLS = P_SIZE * P_SIZE
SPAN = 32
FIELDS = 8
GROUP = 2

SIGMA_LOW = 0.02
SIGMA_HIGH = 80.0
SIGMA_DATA = 0.5
EPSILON = 1e-06
AXES = ("tile", "dp")
BF16 = jnp.bfloat16
F32 = jnp.float32


def sigmoid(values):
    return 0.5 * jnp.tanh(0.5 * values) + 0.5


def from_previous_column(x, col):
    return jnp.where(col == 0, 0.0, pltpu.roll(x, 1, 0))


def from_next_column(x, col):
    return jnp.where(col == P_SIZE - 1, 0.0, pltpu.roll(x, x.shape[0] - 1, 0))


def from_previous_row(x):
    zero = jnp.zeros((P_SIZE, x.shape[1]), x.dtype)
    parts = []
    for at in range(0, x.shape[0], CELLS):
        parts += [zero, x[at : at + CELLS - P_SIZE]]
    return jnp.concatenate(parts, axis=0)


def from_next_row(x):
    zero = jnp.zeros((P_SIZE, x.shape[1]), x.dtype)
    parts = []
    for at in range(0, x.shape[0], CELLS):
        parts += [x[at + P_SIZE : at + CELLS], zero]
    return jnp.concatenate(parts, axis=0)


def store_window(ref, base, tap, rows):
    lanes = pl.ds(tap * C, C)
    shift = tap // 3
    if shift == 0:
        ref[base + P_SIZE : base + CELLS, lanes] = rows[: CELLS - P_SIZE]
    elif shift == 1:
        ref[base : base + CELLS, lanes] = rows
    else:
        ref[base : base + CELLS - P_SIZE, lanes] = rows[P_SIZE:]


def train_kernel(
    dp_count,
    npatch,
    place,
    table_hbm,
    table,
    features,
    target,
    w_a,
    w_u,
    b_a,
    e_a,
    w_b,
    b_b,
    w_o,
    keep_out,
    send_out,
    loss_out,
    ints,
    chosen,
    blocks,
    target32,
    extra32,
    weight_a,
    weight_b,
    win_a,
    act,
    win_g,
    slope,
    aim,
    grad_a,
    grad_b,
    int_sem,
    weight_sems,
    block_sems,
):
    devices = table.shape[0]
    slots = blocks.shape[0]
    taps = 9
    my_tile, my_dp = place[0], place[1]

    copy_ints = pltpu.make_async_copy(table_hbm.at[:, 0, pl.ds(npatch * CELLS, C)], ints, int_sem)
    copy_ints.start()
    copies = [pltpu.make_async_copy(w_a, weight_a.at[pl.ds(0, taps * C)], weight_sems.at[taps])]
    for tap in range(taps):
        copies.append(
            pltpu.make_async_copy(
                w_b.at[pl.ds(tap * HID, HID)],
                weight_b.at[:, pl.ds(tap * C, C)],
                weight_sems.at[tap],
            )
        )
    for copy in copies:
        copy.start()
    copy_ints.wait()

    tile_name = my_tile.astype(F32)

    def choose(device, carry):
        turn, place_at = carry
        for patch in range(npatch):
            owned = ints[device, patch * FIELDS] == tile_name
            mine = jnp.logical_and(owned, turn == my_dp)
            chosen[jnp.where(mine, place_at, slots)] = device * npatch + patch
            place_at = jnp.where(mine, place_at + 1, place_at)
            following = jnp.where(turn == dp_count - 1, 0, turn + 1)
            turn = jnp.where(owned, following, turn)
        return turn, place_at

    _, count = lax.fori_loop(0, devices, choose, (jnp.int32(0), jnp.int32(0)))

    def fields(slot):
        patch = chosen[slot]
        device = lax.div(patch, npatch)
        inner = lax.rem(patch, npatch)
        return device, inner

    def block_copy(slot):
        device, inner = fields(slot)
        row = ints[device, inner * FIELDS + 1].astype(jnp.int32)
        column = ints[device, inner * FIELDS + 2].astype(jnp.int32)
        most = (features.shape[1] - SPAN) // 16
        start = jnp.minimum(lax.shift_right_logical(column, 4), most) * 16
        start = pl.multiple_of(start, 16)
        copy = pltpu.make_async_copy(
            features.at[pl.ds(row, P_SIZE), pl.ds(start, SPAN)],
            blocks.at[slot],
            block_sems.at[slot],
        )
        return copy, row, column, column - start

    def start_block(slot, carry):
        block_copy(slot)[0].start()
        return carry

    lax.fori_loop(0, count, start_block, 0)

    grad_a[...] = jnp.zeros_like(grad_a)
    grad_b[...] = jnp.zeros_like(grad_b)
    loss_out[...] = jnp.zeros_like(loss_out)
    edge = jnp.zeros((P_SIZE, 3 * C), BF16)
    for part in range(GROUP):
        base = part * CELLS
        for ref in (win_a, win_g):
            ref[base : base + P_SIZE, : 3 * C] = edge
            ref[base + CELLS - P_SIZE : base + CELLS, 6 * C : 9 * C] = edge
    target32[...] = target[...].astype(F32)

    def high(value):
        return value.astype(BF16).astype(F32)

    extra32[...] = jnp.zeros_like(extra32)
    w_u_value, b_a_value, e_a_value = w_u[...], b_a[...], e_a[...]
    extra32[0:taps] = high(w_u_value)
    extra32[taps : 2 * taps] = w_u_value - high(w_u_value)
    extra32[2 * taps : 3 * taps] = high(w_u_value)
    extra32[27:28] = high(b_a_value)
    extra32[28:29] = b_a_value - high(b_a_value)
    extra32[29:30] = high(e_a_value)
    extra32[30:31] = e_a_value - high(e_a_value)
    extra32[31:32] = high(e_a_value)
    weight_a[taps * C :] = extra32[...].astype(BF16)
    for copy in copies:
        copy.wait()

    cell_col = lax.broadcasted_iota(jnp.int32, (CELLS, C), 0) & (P_SIZE - 1)
    lane = lax.broadcasted_iota(jnp.int32, (CELLS, C), 1)
    lane_tap = lax.rem(lane, taps)
    lane_row, lane_col = lax.div(lane_tap, 3), lax.rem(lane_tap, 3)
    pick_shape = (P_SIZE, P_SIZE, C)
    pick_row = lax.broadcasted_iota(jnp.int32, pick_shape, 0) & 7
    pick_col = lax.broadcasted_iota(jnp.int32, pick_shape, 1)
    pick_lane = lax.broadcasted_iota(jnp.int32, pick_shape, 2)
    noise_pick = pick_lane == pick_row * P_SIZE + pick_col
    field_shape = (P_SIZE, P_SIZE, target.shape[1])
    field_col = lax.broadcasted_iota(jnp.int32, field_shape, 1)
    field_lane = lax.broadcasted_iota(jnp.int32, field_shape, 2)
    loss_row = lax.broadcasted_iota(jnp.int32, loss_out.shape, 0)
    loss_lane = lax.broadcasted_iota(jnp.int32, loss_out.shape, 1)
    both_col = lax.broadcasted_iota(jnp.int32, (GROUP * CELLS, C), 0) & (P_SIZE - 1)
    log_step = (math.log(SIGMA_HIGH) - math.log(SIGMA_LOW)) / (LEVELS - 1)

    def prepare(part, slot):
        base = part * CELLS
        copy, row, _, offset = block_copy(slot)
        device, inner = fields(slot)
        column = ints[device, inner * FIELDS + 2].astype(jnp.int32)
        level = ints[device, inner * FIELDS + 3]

        span = blocks[slot].astype(F32).reshape(P_SIZE * SPAN, C)
        span = pltpu.roll(span, (P_SIZE * SPAN - offset) & (P_SIZE * SPAN - 1), 0).reshape(P_SIZE, SPAN, C)
        block = span[:, :P_SIZE, :].reshape(CELLS, C)
        for shift, value in enumerate(
            (from_previous_column(block, cell_col), block, from_next_column(block, cell_col))
        ):
            value = value.astype(BF16)
            for shift_row in range(3):
                store_window(win_a, base, 3 * shift_row + shift, value)

        log_sigma = math.log(SIGMA_LOW) + jnp.full((1, 1), level) * log_step
        sigma = jnp.exp(log_sigma)
        variance = sigma * sigma + SIGMA_DATA * SIGMA_DATA
        scale_in = 1.0 / jnp.sqrt(variance)
        embed = jnp.log(sigma) / 4.0

        tile_rows = target.shape[0]
        lines = pltpu.roll(target32[...], lax.rem(tile_rows - row, tile_rows), 0)[:P_SIZE]
        clean = jnp.sum(
            jnp.where(field_lane == column + field_col, lines[:, None, :], 0.0),
            axis=2,
            keepdims=True,
        )
        at = pl.multiple_of(inner * CELLS, C)
        first = table[device, :, pl.ds(at, C)]
        second = table[device, :, pl.ds(pl.multiple_of(at + C, C), C)]
        half = (P_SIZE // 2, P_SIZE, C)
        drawn = jnp.concatenate(
            [jnp.broadcast_to(first[None], half), jnp.broadcast_to(second[None], half)], axis=0
        )
        noise = jnp.sum(jnp.where(noise_pick, drawn, 0.0), axis=2, keepdims=True)
        clean = jnp.broadcast_to(clean, pick_shape).reshape(CELLS, C)
        noise = jnp.broadcast_to(noise, pick_shape).reshape(CELLS, C)
        scaled = scale_in * (clean + sigma * noise)
        aim[base : base + CELLS] = scale_in * (2.0 * sigma * clean - 0.5 * noise)

        rows = jnp.where(
            lane_row == 0,
            from_previous_row(scaled),
            jnp.where(lane_row == 2, from_next_row(scaled), scaled),
        )
        moved = jnp.where(
            lane_col == 0,
            from_previous_column(rows, cell_col),
            jnp.where(lane_col == 2, from_next_column(rows, cell_col), rows),
        )
        moved_high = high(moved)
        value = jnp.where(lane < 2 * taps, moved_high, moved - moved_high)
        embed_high = high(embed)
        rest = jnp.where(
            lane < 29, 1.0, jnp.where(lane < 31, embed_high, embed - embed_high)
        )
        value = jnp.where(lane < 3 * taps, value, jnp.where(lane < 32, rest, 0.0))
        win_a[base : base + CELLS, taps * C :] = value.astype(BF16)

    def work(step, carry):
        slots_at = [step * GROUP + part for part in range(GROUP)]
        real = [slot < count for slot in slots_at]
        used = [jnp.minimum(slot, count - 1) for slot in slots_at]
        for part in range(GROUP):
            @pl.when(real[part])
            def _(part=part):
                block_copy(used[part])[0].wait()

        for part in range(GROUP):
            prepare(part, used[part])
        weights = []
        for part in range(GROUP):
            device, inner = fields(used[part])
            weight = ints[device, inner * FIELDS + 4]
            weights.append(jnp.where(real[part], weight, 0.0))

        for at in range(0, HID, 256):
            lanes = slice(at, at + 256)
            pre_a = jnp.dot(win_a[...], weight_a[:, lanes], preferred_element_type=F32)
            gate = sigmoid(pre_a)
            act[:, lanes] = (pre_a * gate).astype(BF16)
            slope[:, lanes] = gate * (1.0 + pre_a * (1.0 - gate))

        product = jnp.dot(act[...], weight_b[...], preferred_element_type=F32)
        columns = []
        for shift in range(3):
            tap = [product[:, (3 * r + shift) * C : (3 * r + shift + 1) * C] for r in range(3)]
            columns.append(from_previous_row(tap[0]) + tap[1] + from_next_row(tap[2]))
        pre_b = (
            b_b[...]
            + from_previous_column(columns[0], both_col)
            + columns[1]
            + from_next_column(columns[2], both_col)
        )
        gate = sigmoid(pre_b)
        final = jnp.sum(pre_b * gate * w_o[...], axis=1, keepdims=True)
        residual = final - aim[...]
        factors = []
        for part in range(GROUP):
            base = part * CELLS
            mine = residual[base : base + CELLS]
            loss = weights[part] * jnp.sum(mine * mine) * (1.0 / (CELLS * C))
            device, inner = fields(used[part])
            spot = jnp.logical_and(loss_row == device, loss_lane == inner)
            loss_out[...] += jnp.where(spot, loss, 0.0)
            factors.append((2.0 / CELLS) * weights[part] * mine)
        factor = jnp.concatenate(factors, axis=0)
        grad_pre_b = factor * w_o[...] * (gate * (1.0 + pre_b * (1.0 - gate)))
        for shift, value in enumerate(
            (from_next_column(grad_pre_b, both_col), grad_pre_b, from_previous_column(grad_pre_b, both_col))
        ):
            value = value.astype(BF16)
            for part in range(GROUP):
                mine = value[part * CELLS : (part + 1) * CELLS]
                for shift_row in range(3):
                    lanes = pl.ds((3 * shift_row + shift) * C, C)
                    base = part * CELLS
                    if shift_row == 0:
                        win_g[base : base + CELLS - P_SIZE, lanes] = mine[P_SIZE:]
                    elif shift_row == 1:
                        win_g[base : base + CELLS, lanes] = mine
                    else:
                        win_g[base + P_SIZE : base + CELLS, lanes] = mine[: CELLS - P_SIZE]

        over_cells = (((0,), (0,)), ((), ()))
        grad_b[...] += lax.dot_general(
            act[...], win_g[...], over_cells, preferred_element_type=F32
        )
        grad_hidden = lax.dot_general(
            win_g[...], weight_b[...], (((1,), (1,)), ((), ())), preferred_element_type=F32
        )
        grad_pre_a = (grad_hidden * slope[...]).astype(BF16)
        grad_a[...] += lax.dot_general(
            grad_pre_a, win_a[:, : taps * C], over_cells, preferred_element_type=F32
        )
        return carry

    for part in range(GROUP):
        base = part * CELLS
        win_g[base + CELLS - P_SIZE : base + CELLS, : 3 * C] = edge
        win_g[base : base + P_SIZE, 6 * C : 9 * C] = edge
    lax.fori_loop(0, lax.div(count + GROUP - 1, GROUP), work, 0)

    chunk = HID // devices
    my_core = place[2]
    for pair in range(devices // 2):
        for at, grad in ((0, grad_a), (taps * C, grad_b)):
            lanes = pl.ds(at, taps * C)
            even = grad[2 * pair * chunk : (2 * pair + 1) * chunk]
            odd = grad[(2 * pair + 1) * chunk : (2 * pair + 2) * chunk]
            first = my_core == 0
            keep_out[pair, :, lanes] = jnp.where(first, even, odd)
            send_out[pair, :, lanes] = jnp.where(first, odd, even).astype(BF16)


def halve_kernel(fan, count, place, keep, *refs):
    received, outs = refs[:count], refs[count:]
    mine = place[0]
    for peer in range(fan):
        low = jnp.bitwise_xor(mine, peer)
        for high_part in range(keep.shape[0] // fan):
            at = high_part * fan + low
            total = keep[at]
            for other in received:
                total = total + other[at].astype(F32)
            outs[peer][high_part] = total.astype(outs[peer].dtype)


def finish_kernel(npatch, keep, losses, *refs):
    received, (grad, payload) = refs[:-2], refs[-2:]
    total = keep[0]
    for other in received:
        total = total + other[0].astype(F32)
    grad[...] = total
    half = total.shape[1] // 2
    lane = lax.broadcasted_iota(jnp.int32, losses.shape, 1)
    square_a = jnp.sum(total[:, :half] * total[:, :half])
    square_b = jnp.sum(total[:, half:] * total[:, half:])
    value = jnp.where(lane == npatch, square_a, losses[...])
    payload[:, 0, :] = jnp.where(lane == npatch + 1, square_b, value)


def scale_kernel(npatch, entries, grad, payload, losses, upd_a, upd_b):
    total = jnp.sum(payload[:, 0, :], axis=0, keepdims=True)
    lane = lax.broadcasted_iota(jnp.int32, total.shape, 1)
    losses[...] = total
    half = grad.shape[1] // 2
    for part, out in enumerate((upd_a, upd_b)):
        square = jnp.sum(jnp.where(lane == npatch + part, total, 0.0), axis=1, keepdims=True)
        out[...] = grad[:, part * half : (part + 1) * half] / jnp.sqrt(square / entries + EPSILON)


def local(
    features,
    target_field,
    owner_tile,
    row_offset,
    column_start,
    noise_level,
    icing_count,
    noise_draw,
    w_a,
    w_u,
    b_a,
    e_a,
    w_b,
    b_b,
    w_o,
):
    tile_count, dp_count = lax.axis_size("tile"), lax.axis_size("dp")
    devices = tile_count * dp_count
    npatch = owner_tile.shape[0]
    slots = max(2, 2 * npatch // tile_count) * devices // dp_count
    chunk = HID // devices
    width = 2 * 9 * C
    tile, dp = lax.axis_index("tile"), lax.axis_index("dp")
    index = tile * dp_count + dp
    any_space = pl.BlockSpec(memory_space=pl.ANY)
    in_vmem = pl.BlockSpec(memory_space=pltpu.VMEM)
    in_smem = pl.BlockSpec(memory_space=pltpu.SMEM)

    numbers = jnp.stack(
        [owner_tile[:, 0], row_offset, column_start, noise_level, icing_count], axis=1
    ).astype(F32)
    numbers = jnp.pad(numbers, ((0, 0), (0, FIELDS - 5))).reshape(-1)
    numbers = jnp.pad(numbers, (0, C - numbers.shape[0]))
    line = jnp.concatenate([noise_draw.reshape(-1), numbers])
    table = lax.all_to_all(
        jnp.broadcast_to(line[None, None, :], (devices, 1, line.shape[0])),
        AXES,
        split_axis=0,
        concat_axis=0,
        tiled=True,
    )

    place = jnp.stack([tile, dp, lax.rem(index, 2)]).astype(jnp.int32)
    keep, send, losses = pl.pallas_call(
        functools.partial(train_kernel, dp_count, npatch),
        out_shape=(
            jax.ShapeDtypeStruct((devices // 2, chunk, width), F32),
            jax.ShapeDtypeStruct((devices // 2, chunk, width), BF16),
            jax.ShapeDtypeStruct((devices, C), F32),
        ),
        in_specs=[
            in_smem,
            any_space,
            in_vmem,
            any_space,
            in_vmem,
            any_space,
            in_vmem,
            in_vmem,
            in_vmem,
            any_space,
            in_vmem,
            in_vmem,
        ],
        out_specs=(in_vmem, in_vmem, in_vmem),
        scratch_shapes=[
            pltpu.SMEM((devices, C), F32),
            pltpu.SMEM((slots + 1,), jnp.int32),
            pltpu.VMEM((slots, P_SIZE, SPAN, C), BF16),
            pltpu.VMEM(target_field.shape, F32),
            pltpu.VMEM((C, HID), F32),
            pltpu.VMEM((10 * C, HID), BF16),
            pltpu.VMEM((HID, 9 * C), BF16),
            pltpu.VMEM((GROUP * CELLS, 10 * C), BF16),
            pltpu.VMEM((GROUP * CELLS, HID), BF16),
            pltpu.VMEM((GROUP * CELLS, 9 * C), BF16),
            pltpu.VMEM((GROUP * CELLS, HID), F32),
            pltpu.VMEM((GROUP * CELLS, C), F32),
            pltpu.VMEM((HID, 9 * C), F32),
            pltpu.VMEM((HID, 9 * C), F32),
            pltpu.SemaphoreType.DMA,
            pltpu.SemaphoreType.DMA((10,)),
            pltpu.SemaphoreType.DMA((slots,)),
        ],
        compiler_params=pltpu.CompilerParams(vmem_limit_bytes=50 * 1024 * 1024),
        name="train",
    )(
        place,
        table,
        table,
        features,
        target_field,
        w_a,
        w_u,
        b_a.reshape(1, -1),
        e_a.reshape(1, -1),
        w_b,
        b_b.reshape(1, -1),
        w_o.reshape(1, -1),
    )

    def exchange(array, distance):
        return lax.ppermute(array, AXES, [(i, i ^ distance) for i in range(devices)])

    received = [exchange(send, 1)]
    step = 2
    while step < devices:
        fan = min(8, devices // step)
        side = lax.rem(lax.div(index, step), fan).astype(jnp.int32).reshape(1)
        part = (keep.shape[0] // fan, chunk, width)
        outs = pl.pallas_call(
            functools.partial(halve_kernel, fan, len(received)),
            out_shape=(
                jax.ShapeDtypeStruct(part, F32),
                *[jax.ShapeDtypeStruct(part, BF16) for _ in range(fan - 1)],
            ),
            in_specs=[in_smem] + [in_vmem] * (1 + len(received)),
            out_specs=(in_vmem,) * fan,
            compiler_params=pltpu.CompilerParams(vmem_limit_bytes=32 * 1024 * 1024),
            name=f"halve_{step}",
        )(side, keep, *received)
        keep = outs[0]
        received = [exchange(outs[peer], peer * step) for peer in range(1, fan)]
        step *= fan

    grad, payload = pl.pallas_call(
        functools.partial(finish_kernel, npatch),
        out_shape=(
            jax.ShapeDtypeStruct((chunk, width), F32),
            jax.ShapeDtypeStruct((devices, 1, C), F32),
        ),
        in_specs=[in_vmem] * (2 + len(received)),
        out_specs=(in_vmem, in_vmem),
        name="finish",
    )(keep, losses, *received)
    payload = lax.all_to_all(payload, AXES, split_axis=0, concat_axis=0, tiled=True)
    out = jax.ShapeDtypeStruct((chunk, width // 2), F32)
    sums, upd_a, upd_b = pl.pallas_call(
        functools.partial(scale_kernel, npatch, HID * 9 * C),
        out_shape=(jax.ShapeDtypeStruct((1, C), F32), out, out),
        in_specs=[in_vmem, in_vmem],
        out_specs=(in_vmem,) * 3,
        name="scale",
    )(grad, payload)
    return sums[0, :npatch], upd_a, upd_b


def solution(mesh):
    both = P(AXES)
    return jax.shard_map(
        local,
        mesh=mesh,
        in_specs=(
            P("tile", None, None),
            P("tile", None),
            P(AXES, None),
            both,
            both,
            both,
            both,
            P(AXES, None, None),
            P(),
            P(),
            P(),
            P(),
            P(),
            P(),
            P(),
        ),
        out_specs=(both, P(AXES, None), P(AXES, None)),
        check_vma=False,
    )
```

```python
import functools
import math

import jax
import jax.numpy as jnp
from jax import lax
from jax.experimental import pallas as pl
from jax.experimental.pallas import tpu as pltpu
from jax.sharding import PartitionSpec as P

C = 128
HID = 512
P_SIZE = 16
LEVELS = 32
CELLS = P_SIZE * P_SIZE
SPAN = 32
FIELDS = 8
GROUP = 2

SIGMA_LOW = 0.02
SIGMA_HIGH = 80.0
SIGMA_DATA = 0.5
EPSILON = 1e-06
AXES = ("tile", "dp")
BF16 = jnp.bfloat16
F32 = jnp.float32


def sigmoid(values):
    return 0.5 * jnp.tanh(0.5 * values) + 0.5


def from_previous_column(x, col):
    return jnp.where(col == 0, 0.0, pltpu.roll(x, 1, 0))


def from_next_column(x, col):
    return jnp.where(col == P_SIZE - 1, 0.0, pltpu.roll(x, x.shape[0] - 1, 0))


def from_previous_row(x):
    zero = jnp.zeros((P_SIZE, x.shape[1]), x.dtype)
    parts = []
    for at in range(0, x.shape[0], CELLS):
        parts += [zero, x[at : at + CELLS - P_SIZE]]
    return jnp.concatenate(parts, axis=0)


def from_next_row(x):
    zero = jnp.zeros((P_SIZE, x.shape[1]), x.dtype)
    parts = []
    for at in range(0, x.shape[0], CELLS):
        parts += [x[at + P_SIZE : at + CELLS], zero]
    return jnp.concatenate(parts, axis=0)


def high(value):
    return value.astype(BF16).astype(F32)


def store_window(ref, base, tap, rows):
    lanes = pl.ds(tap * C, C)
    shift = tap // 3
    if shift == 0:
        ref[base + P_SIZE : base + CELLS, lanes] = rows[: CELLS - P_SIZE]
    elif shift == 1:
        ref[base : base + CELLS, lanes] = rows
    else:
        ref[base : base + CELLS - P_SIZE, lanes] = rows[P_SIZE:]


def pack_kernel(owner, row, column, level, count, noise, line, drawn, sem):
    copy = pltpu.make_async_copy(noise, drawn, sem)
    copy.start()
    npatch = noise.shape[0]
    lane = lax.broadcasted_iota(jnp.int32, (1, C), 1)
    numbers = jnp.zeros((1, C), jnp.int32)
    for patch in range(npatch):
        values = (owner[patch], row[patch], column[patch], level[patch], count[patch])
        for at, value in enumerate(values):
            numbers = jnp.where(lane == patch * FIELDS + at, value, numbers)
    shape = (line.shape[0], 1, C)
    line[:, :, npatch * CELLS :] = jnp.broadcast_to(numbers.astype(F32)[None], shape)
    copy.wait()
    rows = C // P_SIZE
    mine = lax.broadcasted_iota(jnp.int32, (rows, C), 0)
    here = lax.broadcasted_iota(jnp.int32, (rows, C), 1) // P_SIZE == mine
    for patch in range(npatch):
        for at in range(0, P_SIZE, rows):
            part = drawn[patch, at : at + rows, :]
            spread = jnp.concatenate([part] * rows, axis=1)
            flat = jnp.sum(jnp.where(here, spread, 0.0), axis=0, keepdims=True)
            start = patch * CELLS + at * P_SIZE
            line[:, :, start : start + C] = jnp.broadcast_to(flat[None], shape)


def weights_kernel(
    w_a, w_u, b_a, e_a, w_b, b_b, w_o, target,
    weight_a, weight_b, weight_back, ends, target32,
    small_u, small_b, small_e, extra32, field, sems,
):
    taps = 9
    copies = [
        pltpu.make_async_copy(w_b.at[pl.ds(tap * HID, HID)], weight_b.at[:, pl.ds(tap * C, C)], sems.at[tap])
        for tap in range(taps)
    ]
    places = (
        (w_a, weight_a.at[pl.ds(0, taps * C)]),
        (w_u, small_u),
        (b_a, small_b),
        (e_a, small_e),
        (b_b, ends.at[pl.ds(0, 1)]),
        (w_o, ends.at[pl.ds(1, 1)]),
        (target, field),
    )
    smalls = [pltpu.make_async_copy(src, dst, sems.at[taps + at]) for at, (src, dst) in enumerate(places)]
    for copy in smalls + copies:
        copy.start()
    for copy in smalls[1:]:
        copy.wait()
    target32[...] = field[...].astype(F32)
    extra32[...] = jnp.zeros_like(extra32)
    w_u_value, b_a_value, e_a_value = small_u[...], small_b[...], small_e[...]
    extra32[0:taps] = high(w_u_value)
    extra32[taps : 2 * taps] = w_u_value - high(w_u_value)
    extra32[2 * taps : 3 * taps] = high(w_u_value)
    extra32[27:28] = high(b_a_value)
    extra32[28:29] = b_a_value - high(b_a_value)
    extra32[29:30] = high(e_a_value)
    extra32[30:31] = e_a_value - high(e_a_value)
    extra32[31:32] = high(e_a_value)
    weight_a[taps * C :] = extra32[...].astype(BF16)
    for tap, copy in enumerate(copies):
        copy.wait()
        weight_back[tap * C : (tap + 1) * C, :] = weight_b[:, tap * C : (tap + 1) * C].T
    smalls[0].wait()


def train_kernel(
    dp_count,
    npatch,
    table_hbm,
    table,
    features,
    target32_hbm,
    weight_a_hbm,
    weight_b_hbm,
    weight_back_hbm,
    ends_hbm,
    keep_out,
    send_out,
    loss_out,
    ints,
    chosen,
    blocks,
    target32,
    weight_a,
    weight_b,
    weight_back,
    ends,
    win_a,
    act,
    win_g,
    slope,
    aim,
    grad_a,
    grad_b,
    int_sem,
    weight_sems,
    block_sems,
):
    devices = table.shape[0]
    slots = blocks.shape[0]
    taps = 9
    my_tile, my_dp = lax.axis_index("tile"), lax.axis_index("dp")
    my_core = lax.rem(my_tile * dp_count + my_dp, 2)

    copy_ints = pltpu.make_async_copy(table_hbm.at[:, 0, pl.ds(npatch * CELLS, C)], ints, int_sem)
    copy_ints.start()
    operands = (
        (target32_hbm, target32),
        (ends_hbm, ends),
        (weight_a_hbm, weight_a),
        (weight_b_hbm, weight_b),
        (weight_back_hbm, weight_back),
    )
    copies = [pltpu.make_async_copy(src, dst, weight_sems.at[at]) for at, (src, dst) in enumerate(operands)]
    copy_ints.wait()

    tile_name = my_tile.astype(F32)

    def choose(device, carry):
        turn, place_at = carry
        for patch in range(npatch):
            owned = ints[device, patch * FIELDS] == tile_name
            mine = jnp.logical_and(owned, turn == my_dp)
            chosen[jnp.where(mine, place_at, slots)] = device * npatch + patch
            place_at = jnp.where(mine, place_at + 1, place_at)
            following = jnp.where(turn == dp_count - 1, 0, turn + 1)
            turn = jnp.where(owned, following, turn)
        return turn, place_at

    _, count = lax.fori_loop(0, devices, choose, (jnp.int32(0), jnp.int32(0)))

    def fields(slot):
        patch = chosen[slot]
        device = lax.div(patch, npatch)
        inner = lax.rem(patch, npatch)
        return device, inner

    def block_copy(slot):
        device, inner = fields(slot)
        row = ints[device, inner * FIELDS + 1].astype(jnp.int32)
        column = ints[device, inner * FIELDS + 2].astype(jnp.int32)
        most = (features.shape[1] - SPAN) // 16
        start = jnp.minimum(lax.shift_right_logical(column, 4), most) * 16
        start = pl.multiple_of(start, 16)
        copy = pltpu.make_async_copy(
            features.at[pl.ds(row, P_SIZE), pl.ds(start, SPAN)],
            blocks.at[slot],
            block_sems.at[slot],
        )
        return copy, row, column, column - start

    def start_block(slot, carry):
        block_copy(slot)[0].start()
        return carry

    lax.fori_loop(0, count, start_block, 0)
    for copy in copies:
        copy.start()

    @pl.when(count == 0)
    def _():
        grad_a[...] = jnp.zeros_like(grad_a)
        grad_b[...] = jnp.zeros_like(grad_b)

    loss_out[...] = jnp.zeros_like(loss_out)
    edge = jnp.zeros((P_SIZE, 3 * C), BF16)
    for part in range(GROUP):
        first, last = part * CELLS, (part + 1) * CELLS - P_SIZE
        win_a[first : first + P_SIZE, : 3 * C] = edge
        win_a[last : last + P_SIZE, 6 * C : 9 * C] = edge
        win_g[last : last + P_SIZE, : 3 * C] = edge
        win_g[first : first + P_SIZE, 6 * C : 9 * C] = edge

    for copy in copies:
        copy.wait()

    cell_col = lax.broadcasted_iota(jnp.int32, (CELLS, C), 0) & (P_SIZE - 1)
    lane = lax.broadcasted_iota(jnp.int32, (CELLS, C), 1)
    lane_tap = lax.rem(lane, taps)
    lane_row, lane_col = lax.div(lane_tap, 3), lax.rem(lane_tap, 3)
    pick_shape = (P_SIZE, P_SIZE, C)
    pick_row = lax.broadcasted_iota(jnp.int32, pick_shape, 0) & 7
    pick_col = lax.broadcasted_iota(jnp.int32, pick_shape, 1)
    pick_lane = lax.broadcasted_iota(jnp.int32, pick_shape, 2)
    noise_pick = pick_lane == pick_row * P_SIZE + pick_col
    field_shape = (P_SIZE, P_SIZE, target32.shape[1])
    field_col = lax.broadcasted_iota(jnp.int32, field_shape, 1)
    field_lane = lax.broadcasted_iota(jnp.int32, field_shape, 2)
    loss_row = lax.broadcasted_iota(jnp.int32, loss_out.shape, 0)
    loss_lane = lax.broadcasted_iota(jnp.int32, loss_out.shape, 1)
    both_col = lax.broadcasted_iota(jnp.int32, (GROUP * CELLS, C), 0) & (P_SIZE - 1)
    log_step = (math.log(SIGMA_HIGH) - math.log(SIGMA_LOW)) / (LEVELS - 1)

    def prepare(part, slot):
        base = part * CELLS
        copy, row, _, offset = block_copy(slot)
        device, inner = fields(slot)
        column = ints[device, inner * FIELDS + 2].astype(jnp.int32)
        level = ints[device, inner * FIELDS + 3]

        span = blocks[slot].astype(F32).reshape(P_SIZE * SPAN, C)
        span = pltpu.roll(span, (P_SIZE * SPAN - offset) & (P_SIZE * SPAN - 1), 0).reshape(P_SIZE, SPAN, C)
        block = span[:, :P_SIZE, :].reshape(CELLS, C)
        for shift, value in enumerate(
            (from_previous_column(block, cell_col), block, from_next_column(block, cell_col))
        ):
            value = value.astype(BF16)
            for shift_row in range(3):
                store_window(win_a, base, 3 * shift_row + shift, value)

        log_sigma = math.log(SIGMA_LOW) + jnp.full((1, 1), level) * log_step
        sigma = jnp.exp(log_sigma)
        variance = sigma * sigma + SIGMA_DATA * SIGMA_DATA
        scale_in = 1.0 / jnp.sqrt(variance)
        embed = jnp.log(sigma) / 4.0

        tile_rows = target32.shape[0]
        lines = pltpu.roll(target32[...], lax.rem(tile_rows - row, tile_rows), 0)[:P_SIZE]
        clean = jnp.sum(
            jnp.where(field_lane == column + field_col, lines[:, None, :], 0.0),
            axis=2,
            keepdims=True,
        )
        at = pl.multiple_of(inner * CELLS, C)
        first = table[device, :, pl.ds(at, C)]
        second = table[device, :, pl.ds(pl.multiple_of(at + C, C), C)]
        half = (P_SIZE // 2, P_SIZE, C)
        drawn = jnp.concatenate(
            [jnp.broadcast_to(first[None], half), jnp.broadcast_to(second[None], half)], axis=0
        )
        noise = jnp.sum(jnp.where(noise_pick, drawn, 0.0), axis=2, keepdims=True)
        clean = jnp.broadcast_to(clean, pick_shape).reshape(CELLS, C)
        noise = jnp.broadcast_to(noise, pick_shape).reshape(CELLS, C)
        scaled = scale_in * (clean + sigma * noise)
        aim[base : base + CELLS] = scale_in * (2.0 * sigma * clean - 0.5 * noise)

        rows = jnp.where(
            lane_row == 0,
            from_previous_row(scaled),
            jnp.where(lane_row == 2, from_next_row(scaled), scaled),
        )
        moved = jnp.where(
            lane_col == 0,
            from_previous_column(rows, cell_col),
            jnp.where(lane_col == 2, from_next_column(rows, cell_col), rows),
        )
        moved_high = high(moved)
        value = jnp.where(lane < 2 * taps, moved_high, moved - moved_high)
        embed_high = high(embed)
        rest = jnp.where(
            lane < 29, 1.0, jnp.where(lane < 31, embed_high, embed - embed_high)
        )
        value = jnp.where(lane < 3 * taps, value, jnp.where(lane < 32, rest, 0.0))
        win_a[base : base + CELLS, taps * C :] = value.astype(BF16)

    def work(step, carry):
        slots_at = [step * GROUP + part for part in range(GROUP)]
        real = [slot < count for slot in slots_at]
        used = [jnp.minimum(slot, count - 1) for slot in slots_at]
        for part in range(GROUP):
            @pl.when(real[part])
            def _(part=part):
                block_copy(used[part])[0].wait()

        for part in range(GROUP):
            prepare(part, used[part])
        weights = []
        for part in range(GROUP):
            device, inner = fields(used[part])
            weight = ints[device, inner * FIELDS + 4]
            weights.append(jnp.where(real[part], weight, 0.0))

        for at in range(0, HID, 256):
            lanes = slice(at, at + 256)
            pre_a = jnp.dot(win_a[...], weight_a[:, lanes], preferred_element_type=F32)
            gate = sigmoid(pre_a)
            act[:, lanes] = (pre_a * gate).astype(BF16)
            slope[:, lanes] = gate * (1.0 + pre_a * (1.0 - gate))

        product = jnp.dot(act[...], weight_b[...], preferred_element_type=F32)
        columns = []
        for shift in range(3):
            tap = [product[:, (3 * r + shift) * C : (3 * r + shift + 1) * C] for r in range(3)]
            columns.append(from_previous_row(tap[0]) + tap[1] + from_next_row(tap[2]))
        pre_b = (
            ends[0:1]
            + from_previous_column(columns[0], both_col)
            + columns[1]
            + from_next_column(columns[2], both_col)
        )
        gate = sigmoid(pre_b)
        final = jnp.sum(pre_b * gate * ends[1:2], axis=1, keepdims=True)
        residual = final - aim[...]
        factors = []
        for part in range(GROUP):
            base = part * CELLS
            mine = residual[base : base + CELLS]
            loss = weights[part] * jnp.sum(mine * mine) * (1.0 / (CELLS * C))
            device, inner = fields(used[part])
            spot = jnp.logical_and(loss_row == device, loss_lane == inner)
            loss_out[...] += jnp.where(spot, loss, 0.0)
            factors.append((2.0 / CELLS) * weights[part] * mine)
        factor = jnp.concatenate(factors, axis=0)
        grad_pre_b = factor * ends[1:2] * (gate * (1.0 + pre_b * (1.0 - gate)))
        for shift, value in enumerate(
            (from_next_column(grad_pre_b, both_col), grad_pre_b, from_previous_column(grad_pre_b, both_col))
        ):
            value = value.astype(BF16)
            for part in range(GROUP):
                mine = value[part * CELLS : (part + 1) * CELLS]
                for shift_row in range(3):
                    lanes = pl.ds((3 * shift_row + shift) * C, C)
                    base = part * CELLS
                    if shift_row == 0:
                        win_g[base : base + CELLS - P_SIZE, lanes] = mine[P_SIZE:]
                    elif shift_row == 1:
                        win_g[base : base + CELLS, lanes] = mine
                    else:
                        win_g[base + P_SIZE : base + CELLS, lanes] = mine[: CELLS - P_SIZE]

        over_cells = (((0,), (0,)), ((), ()))
        started = step > 0
        grad_b[...] = jnp.where(started, grad_b[...], 0.0) + lax.dot_general(
            act[...], win_g[...], over_cells, preferred_element_type=F32
        )
        grad_hidden = jnp.dot(win_g[...], weight_back[...], preferred_element_type=F32)
        grad_pre_a = (grad_hidden * slope[...]).astype(BF16)
        grad_a[...] = jnp.where(started, grad_a[...], 0.0) + lax.dot_general(
            grad_pre_a, win_a[:, : taps * C], over_cells, preferred_element_type=F32
        )
        return carry

    lax.fori_loop(0, lax.div(count + GROUP - 1, GROUP), work, 0)

    chunk = HID // devices
    for pair in range(devices // 2):
        for at, grad in ((0, grad_a), (taps * C, grad_b)):
            lanes = pl.ds(at, taps * C)
            even = grad[2 * pair * chunk : (2 * pair + 1) * chunk]
            odd = grad[(2 * pair + 1) * chunk : (2 * pair + 2) * chunk]
            first = my_core == 0
            keep_out[pair, :, lanes] = jnp.where(first, even, odd)
            send_out[pair, :, lanes] = jnp.where(first, odd, even).astype(BF16)


def halve_kernel(fan, count, step, keep, *refs):
    received, outs = refs[:count], refs[count:]
    index = lax.axis_index("tile") * lax.axis_size("dp") + lax.axis_index("dp")
    mine = lax.rem(lax.div(index, step), fan)
    for peer in range(fan):
        low = jnp.bitwise_xor(mine, peer)
        for high_part in range(keep.shape[0] // fan):
            at = high_part * fan + low
            total = keep[at]
            for other in received:
                total = total + other[at].astype(F32)
            outs[peer][high_part] = total.astype(outs[peer].dtype)


def finish_kernel(npatch, keep, losses, *refs):
    received, (grad, payload) = refs[:-2], refs[-2:]
    total = keep[0]
    for other in received:
        total = total + other[0].astype(F32)
    grad[...] = total
    half = total.shape[1] // 2
    lane = lax.broadcasted_iota(jnp.int32, losses.shape, 1)
    square_a = jnp.sum(total[:, :half] * total[:, :half])
    square_b = jnp.sum(total[:, half:] * total[:, half:])
    value = jnp.where(lane == npatch, square_a, losses[...])
    payload[:, 0, :] = jnp.where(lane == npatch + 1, square_b, value)


def scale_kernel(npatch, entries, grad, payload, losses, upd_a, upd_b):
    total = jnp.sum(payload[:, 0, :], axis=0, keepdims=True)
    lane = lax.broadcasted_iota(jnp.int32, total.shape, 1)
    for patch in range(npatch):
        losses[patch] = jnp.sum(jnp.where(lane == patch, total, 0.0))
    half = grad.shape[1] // 2
    for part, out in enumerate((upd_a, upd_b)):
        square = jnp.sum(jnp.where(lane == npatch + part, total, 0.0), axis=1, keepdims=True)
        out[...] = grad[:, part * half : (part + 1) * half] / jnp.sqrt(square / entries + EPSILON)


def local(
    features,
    target_field,
    owner_tile,
    row_offset,
    column_start,
    noise_level,
    icing_count,
    noise_draw,
    w_a,
    w_u,
    b_a,
    e_a,
    w_b,
    b_b,
    w_o,
):
    tile_count, dp_count = lax.axis_size("tile"), lax.axis_size("dp")
    devices = tile_count * dp_count
    npatch = owner_tile.shape[0]
    slots = max(2, 2 * npatch // tile_count) * devices // dp_count
    chunk = HID // devices
    width = 2 * 9 * C
    in_hbm = pl.BlockSpec(memory_space=pltpu.HBM)
    stay = functools.partial(pltpu.with_memory_space_constraint, memory_space=pltpu.HBM)
    in_vmem = pl.BlockSpec(memory_space=pltpu.VMEM)
    in_smem = pl.BlockSpec(memory_space=pltpu.SMEM)

    def room(mebibytes):
        return pltpu.CompilerParams(vmem_limit_bytes=mebibytes * 1024 * 1024)

    line = pl.pallas_call(
        pack_kernel,
        out_shape=jax.ShapeDtypeStruct((devices, 1, npatch * CELLS + C), F32),
        in_specs=[in_smem] * 5 + [in_hbm],
        out_specs=in_vmem,
        scratch_shapes=[pltpu.VMEM(noise_draw.shape, F32), pltpu.SemaphoreType.DMA],
        compiler_params=room(4),
        name="pack",
    )(
        *map(stay, (owner_tile.reshape(-1), row_offset, column_start, noise_level, icing_count, noise_draw))
    )
    table = lax.all_to_all(line, AXES, split_axis=0, concat_axis=0, tiled=True)

    weights = pl.pallas_call(
        weights_kernel,
        out_shape=(
            pltpu.HBM((10 * C, HID), BF16),
            pltpu.HBM((HID, 9 * C), BF16),
            pltpu.HBM((9 * C, HID), BF16),
            pltpu.HBM((2, C), F32),
            pltpu.HBM(target_field.shape, F32),
        ),
        in_specs=[in_hbm] * 8,
        out_specs=(in_vmem,) * 5,
        scratch_shapes=[
            pltpu.VMEM((9, HID), F32),
            pltpu.VMEM((1, HID), F32),
            pltpu.VMEM((1, HID), F32),
            pltpu.VMEM((C, HID), F32),
            pltpu.VMEM(target_field.shape, BF16),
            pltpu.SemaphoreType.DMA((16,)),
        ],
        compiler_params=room(8),
        name="weights",
    )(
        stay(w_a),
        stay(w_u),
        stay(b_a.reshape(1, -1)),
        stay(e_a.reshape(1, -1)),
        stay(w_b),
        stay(b_b.reshape(1, -1)),
        stay(w_o.reshape(1, -1)),
        stay(target_field),
    )
    weight_a, weight_b, weight_back, ends, target32 = weights

    keep, send, losses = pl.pallas_call(
        functools.partial(train_kernel, dp_count, npatch),
        out_shape=(
            pltpu.VMEM((devices // 2, chunk, width), F32),
            pltpu.VMEM((devices // 2, chunk, width), BF16),
            pltpu.VMEM((devices, C), F32),
        ),
        in_specs=[in_hbm, in_vmem] + [in_hbm] * 6,
        out_specs=(in_vmem, in_vmem, in_vmem),
        scratch_shapes=[
            pltpu.SMEM((devices, C), F32),
            pltpu.SMEM((slots + 1,), jnp.int32),
            pltpu.VMEM((slots, P_SIZE, SPAN, C), BF16),
            pltpu.VMEM(target_field.shape, F32),
            pltpu.VMEM((10 * C, HID), BF16),
            pltpu.VMEM((HID, 9 * C), BF16),
            pltpu.VMEM((9 * C, HID), BF16),
            pltpu.VMEM((2, C), F32),
            pltpu.VMEM((GROUP * CELLS, 10 * C), BF16),
            pltpu.VMEM((GROUP * CELLS, HID), BF16),
            pltpu.VMEM((GROUP * CELLS, 9 * C), BF16),
            pltpu.VMEM((GROUP * CELLS, HID), F32),
            pltpu.VMEM((GROUP * CELLS, C), F32),
            pltpu.VMEM((HID, 9 * C), F32),
            pltpu.VMEM((HID, 9 * C), F32),
            pltpu.SemaphoreType.DMA,
            pltpu.SemaphoreType.DMA((5,)),
            pltpu.SemaphoreType.DMA((slots,)),
        ],
        compiler_params=room(32),
        name="train",
    )(table, table, *map(stay, (features, target32, weight_a, weight_b, weight_back, ends)))

    def exchange(array, distance):
        return lax.ppermute(array, AXES, [(i, i ^ distance) for i in range(devices)])

    received = [exchange(send, 1)]
    step = 2
    while step < devices:
        fan = min(8, devices // step)
        part = (keep.shape[0] // fan, chunk, width)
        outs = pl.pallas_call(
            functools.partial(halve_kernel, fan, len(received), step),
            out_shape=(
                pltpu.VMEM(part, F32),
                *[pltpu.VMEM(part, BF16) for _ in range(fan - 1)],
            ),
            in_specs=[in_vmem] * (1 + len(received)),
            out_specs=(in_vmem,) * fan,
            compiler_params=room(8),
            name=f"halve_{step}",
        )(keep, *received)
        keep = outs[0]
        order = sorted(range(1, fan), key=lambda peer: (-peer.bit_count(), -peer))
        received = [exchange(outs[peer], peer * step) for peer in order]
        step *= fan

    grad, payload = pl.pallas_call(
        functools.partial(finish_kernel, npatch),
        out_shape=(
            pltpu.VMEM((chunk, width), F32),
            pltpu.VMEM((devices, 1, C), F32),
        ),
        in_specs=[in_vmem] * (2 + len(received)),
        out_specs=(in_vmem, in_vmem),
        compiler_params=room(4),
        name="finish",
    )(keep, losses, *received)
    payload = lax.all_to_all(payload, AXES, split_axis=0, concat_axis=0, tiled=True)
    out = jax.ShapeDtypeStruct((chunk, width // 2), F32)
    sums, upd_a, upd_b = pl.pallas_call(
        functools.partial(scale_kernel, npatch, HID * 9 * C),
        out_shape=(jax.ShapeDtypeStruct((npatch,), F32), out, out),
        in_specs=[in_vmem, in_vmem],
        out_specs=(in_smem, in_vmem, in_vmem),
        compiler_params=room(4),
        name="scale",
    )(grad, payload)
    return sums, upd_a, upd_b


def solution(mesh):
    both = P(AXES)
    return jax.shard_map(
        local,
        mesh=mesh,
        in_specs=(
            P("tile", None, None),
            P("tile", None),
            P(AXES, None),
            both,
            both,
            both,
            both,
            P(AXES, None, None),
            P(),
            P(),
            P(),
            P(),
            P(),
            P(),
            P(),
        ),
        out_specs=(both, P(AXES, None), P(AXES, None)),
        check_vma=False,
    )
```

```python
import functools
import math

import jax
import jax.numpy as jnp
from jax import lax
from jax.experimental import pallas as pl
from jax.experimental.pallas import tpu as pltpu
from jax.sharding import PartitionSpec as P

C = 128
HID = 512
P_SIZE = 16
LEVELS = 32
CELLS = P_SIZE * P_SIZE
SPAN = 32
FIELDS = 8
GROUP = 2

SIGMA_LOW = 0.02
SIGMA_HIGH = 80.0
SIGMA_DATA = 0.5
EPSILON = 1e-06
AXES = ("tile", "dp")
BF16 = jnp.bfloat16
F32 = jnp.float32


def sigmoid(values):
    return 0.5 * jnp.tanh(0.5 * values) + 0.5


def from_previous_column(x, col):
    return jnp.where(col == 0, 0.0, pltpu.roll(x, 1, 0))


def from_next_column(x, col):
    return jnp.where(col == P_SIZE - 1, 0.0, pltpu.roll(x, x.shape[0] - 1, 0))


def from_previous_row(x):
    zero = jnp.zeros((P_SIZE, x.shape[1]), x.dtype)
    parts = []
    for at in range(0, x.shape[0], CELLS):
        parts += [zero, x[at : at + CELLS - P_SIZE]]
    return jnp.concatenate(parts, axis=0)


def from_next_row(x):
    zero = jnp.zeros((P_SIZE, x.shape[1]), x.dtype)
    parts = []
    for at in range(0, x.shape[0], CELLS):
        parts += [x[at + P_SIZE : at + CELLS], zero]
    return jnp.concatenate(parts, axis=0)


def high(value):
    return value.astype(BF16).astype(F32)


def store_window(ref, base, tap, rows):
    lanes = pl.ds(tap * C, C)
    shift = tap // 3
    if shift == 0:
        ref[base + P_SIZE : base + CELLS, lanes] = rows[: CELLS - P_SIZE]
    elif shift == 1:
        ref[base : base + CELLS, lanes] = rows
    else:
        ref[base : base + CELLS - P_SIZE, lanes] = rows[P_SIZE:]


def pack_kernel(*refs):
    sources, line, scratch, sems = refs[:6], refs[6], refs[7:13], refs[13]
    copies = [
        pltpu.make_async_copy(src, dst, sems.at[at]) for at, (src, dst) in enumerate(zip(sources, scratch))
    ]
    for copy in copies:
        copy.start()
    *integers, drawn = scratch
    npatch = drawn.shape[0]
    lane = lax.broadcasted_iota(jnp.int32, (1, C), 1)
    numbers = jnp.zeros((1, C), jnp.int32)
    for copy in copies:
        copy.wait()
    for patch in range(npatch):
        for at, ref in enumerate(integers):
            numbers = jnp.where(lane == patch * FIELDS + at, ref[patch], numbers)
    shape = (line.shape[0], 1, C)
    line[:, :, npatch * CELLS :] = jnp.broadcast_to(numbers.astype(F32)[None], shape)
    rows = C // P_SIZE
    mine = lax.broadcasted_iota(jnp.int32, (rows, C), 0)
    here = lax.broadcasted_iota(jnp.int32, (rows, C), 1) // P_SIZE == mine
    for patch in range(npatch):
        for at in range(0, P_SIZE, rows):
            part = drawn[patch, at : at + rows, :]
            spread = jnp.concatenate([part] * rows, axis=1)
            flat = jnp.sum(jnp.where(here, spread, 0.0), axis=0, keepdims=True)
            start = patch * CELLS + at * P_SIZE
            line[:, :, start : start + C] = jnp.broadcast_to(flat[None], shape)


def weights_kernel(
    w_a, w_u, b_a, e_a, w_b, b_b, w_o, target,
    weight_a, weight_b, weight_back, ends, target32,
    small_u, small_b, small_e, extra32, field, sems,
):
    taps = 9
    copies = [
        pltpu.make_async_copy(w_b.at[pl.ds(tap * HID, HID)], weight_b.at[:, pl.ds(tap * C, C)], sems.at[tap])
        for tap in range(taps)
    ]
    places = (
        (w_a, weight_a.at[pl.ds(0, taps * C)]),
        (w_u, small_u),
        (b_a, small_b),
        (e_a, small_e),
        (b_b, ends.at[pl.ds(0, 1)]),
        (w_o, ends.at[pl.ds(1, 1)]),
        (target, field),
    )
    smalls = [pltpu.make_async_copy(src, dst, sems.at[taps + at]) for at, (src, dst) in enumerate(places)]
    for copy in smalls + copies:
        copy.start()
    for copy in smalls[1:]:
        copy.wait()
    target32[...] = field[...].astype(F32)
    extra32[...] = jnp.zeros_like(extra32)
    w_u_value, b_a_value, e_a_value = small_u[...], small_b[...], small_e[...]
    extra32[0:taps] = high(w_u_value)
    extra32[taps : 2 * taps] = w_u_value - high(w_u_value)
    extra32[2 * taps : 3 * taps] = high(w_u_value)
    extra32[27:28] = high(b_a_value)
    extra32[28:29] = b_a_value - high(b_a_value)
    extra32[29:30] = high(e_a_value)
    extra32[30:31] = e_a_value - high(e_a_value)
    extra32[31:32] = high(e_a_value)
    weight_a[taps * C :] = extra32[...].astype(BF16)
    for tap, copy in enumerate(copies):
        copy.wait()
        weight_back[tap * C : (tap + 1) * C, :] = weight_b[:, tap * C : (tap + 1) * C].T
    smalls[0].wait()


def train_kernel(
    dp_count,
    npatch,
    table_hbm,
    table,
    features,
    target32_hbm,
    weight_a_hbm,
    weight_b_hbm,
    weight_back_hbm,
    ends_hbm,
    keep_out,
    send_out,
    loss_out,
    ints,
    chosen,
    blocks,
    target32,
    weight_a,
    weight_b,
    weight_back,
    ends,
    win_a,
    act,
    win_g,
    slope,
    aim,
    grad_a,
    grad_b,
    int_sem,
    weight_sems,
    block_sems,
):
    devices = table.shape[0]
    slots = blocks.shape[0]
    taps = 9
    my_tile, my_dp = lax.axis_index("tile"), lax.axis_index("dp")
    my_core = lax.rem(my_tile * dp_count + my_dp, 2)

    copy_ints = pltpu.make_async_copy(table_hbm.at[:, 0, pl.ds(npatch * CELLS, C)], ints, int_sem)
    copy_ints.start()
    operands = (
        (target32_hbm, target32),
        (ends_hbm, ends),
        (weight_a_hbm, weight_a),
        (weight_b_hbm, weight_b),
        (weight_back_hbm, weight_back),
    )
    copies = [pltpu.make_async_copy(src, dst, weight_sems.at[at]) for at, (src, dst) in enumerate(operands)]
    for copy in copies:
        copy.start()
    copy_ints.wait()

    tile_name = my_tile.astype(F32)

    def choose(device, carry):
        turn, place_at = carry
        for patch in range(npatch):
            owned = ints[device, patch * FIELDS] == tile_name
            mine = jnp.logical_and(owned, turn == my_dp)
            chosen[jnp.where(mine, place_at, slots)] = device * npatch + patch
            place_at = jnp.where(mine, place_at + 1, place_at)
            following = jnp.where(turn == dp_count - 1, 0, turn + 1)
            turn = jnp.where(owned, following, turn)
        return turn, place_at

    _, count = lax.fori_loop(0, devices, choose, (jnp.int32(0), jnp.int32(0)))

    def fields(slot):
        patch = chosen[slot]
        device = lax.div(patch, npatch)
        inner = lax.rem(patch, npatch)
        return device, inner

    def block_copy(slot):
        device, inner = fields(slot)
        row = ints[device, inner * FIELDS + 1].astype(jnp.int32)
        column = ints[device, inner * FIELDS + 2].astype(jnp.int32)
        most = (features.shape[1] - SPAN) // 16
        start = jnp.minimum(lax.shift_right_logical(column, 4), most) * 16
        start = pl.multiple_of(start, 16)
        copy = pltpu.make_async_copy(
            features.at[pl.ds(row, P_SIZE), pl.ds(start, SPAN)],
            blocks.at[slot],
            block_sems.at[slot],
        )
        return copy, row, column, column - start

    def start_block(slot, carry):
        block_copy(slot)[0].start()
        return carry

    lax.fori_loop(0, count, start_block, 0)

    @pl.when(count == 0)
    def _():
        grad_a[...] = jnp.zeros_like(grad_a)
        grad_b[...] = jnp.zeros_like(grad_b)

    loss_out[...] = jnp.zeros_like(loss_out)
    edge = jnp.zeros((P_SIZE, 3 * C), BF16)
    for part in range(GROUP):
        first, last = part * CELLS, (part + 1) * CELLS - P_SIZE
        win_a[first : first + P_SIZE, : 3 * C] = edge
        win_a[last : last + P_SIZE, 6 * C : 9 * C] = edge
        win_g[last : last + P_SIZE, : 3 * C] = edge
        win_g[first : first + P_SIZE, 6 * C : 9 * C] = edge

    for copy in copies:
        copy.wait()

    cell_col = lax.broadcasted_iota(jnp.int32, (CELLS, C), 0) & (P_SIZE - 1)
    lane = lax.broadcasted_iota(jnp.int32, (CELLS, C), 1)
    lane_tap = lax.rem(lane, taps)
    lane_row, lane_col = lax.div(lane_tap, 3), lax.rem(lane_tap, 3)
    pick_shape = (P_SIZE, P_SIZE, C)
    pick_row = lax.broadcasted_iota(jnp.int32, pick_shape, 0) & 7
    pick_col = lax.broadcasted_iota(jnp.int32, pick_shape, 1)
    pick_lane = lax.broadcasted_iota(jnp.int32, pick_shape, 2)
    noise_pick = pick_lane == pick_row * P_SIZE + pick_col
    field_shape = (P_SIZE, P_SIZE, target32.shape[1])
    field_col = lax.broadcasted_iota(jnp.int32, field_shape, 1)
    field_lane = lax.broadcasted_iota(jnp.int32, field_shape, 2)
    loss_row = lax.broadcasted_iota(jnp.int32, loss_out.shape, 0)
    loss_lane = lax.broadcasted_iota(jnp.int32, loss_out.shape, 1)
    log_step = (math.log(SIGMA_HIGH) - math.log(SIGMA_LOW)) / (LEVELS - 1)

    def prepare(part, slot):
        base = part * CELLS
        copy, row, _, offset = block_copy(slot)
        device, inner = fields(slot)
        column = ints[device, inner * FIELDS + 2].astype(jnp.int32)
        level = ints[device, inner * FIELDS + 3]

        span = blocks[slot].astype(F32).reshape(P_SIZE * SPAN, C)
        span = pltpu.roll(span, (P_SIZE * SPAN - offset) & (P_SIZE * SPAN - 1), 0).reshape(P_SIZE, SPAN, C)
        block = span[:, :P_SIZE, :].reshape(CELLS, C)
        for shift, value in enumerate(
            (from_previous_column(block, cell_col), block, from_next_column(block, cell_col))
        ):
            value = value.astype(BF16)
            for shift_row in range(3):
                store_window(win_a, base, 3 * shift_row + shift, value)

        log_sigma = math.log(SIGMA_LOW) + jnp.full((1, 1), level) * log_step
        sigma = jnp.exp(log_sigma)
        variance = sigma * sigma + SIGMA_DATA * SIGMA_DATA
        scale_in = 1.0 / jnp.sqrt(variance)
        embed = jnp.log(sigma) / 4.0

        tile_rows = target32.shape[0]
        lines = pltpu.roll(target32[...], lax.rem(tile_rows - row, tile_rows), 0)[:P_SIZE]
        clean = jnp.sum(
            jnp.where(field_lane == column + field_col, lines[:, None, :], 0.0),
            axis=2,
            keepdims=True,
        )
        at = pl.multiple_of(inner * CELLS, C)
        first = table[device, :, pl.ds(at, C)]
        second = table[device, :, pl.ds(pl.multiple_of(at + C, C), C)]
        half = (P_SIZE // 2, P_SIZE, C)
        drawn = jnp.concatenate(
            [jnp.broadcast_to(first[None], half), jnp.broadcast_to(second[None], half)], axis=0
        )
        noise = jnp.sum(jnp.where(noise_pick, drawn, 0.0), axis=2, keepdims=True)
        clean = jnp.broadcast_to(clean, pick_shape).reshape(CELLS, C)
        noise = jnp.broadcast_to(noise, pick_shape).reshape(CELLS, C)
        scaled = scale_in * (clean + sigma * noise)
        aim[base : base + CELLS] = scale_in * (2.0 * sigma * clean - 0.5 * noise)

        rows = jnp.where(
            lane_row == 0,
            from_previous_row(scaled),
            jnp.where(lane_row == 2, from_next_row(scaled), scaled),
        )
        moved = jnp.where(
            lane_col == 0,
            from_previous_column(rows, cell_col),
            jnp.where(lane_col == 2, from_next_column(rows, cell_col), rows),
        )
        moved_high = high(moved)
        value = jnp.where(lane < 2 * taps, moved_high, moved - moved_high)
        embed_high = high(embed)
        rest = jnp.where(
            lane < 29, 1.0, jnp.where(lane < 31, embed_high, embed - embed_high)
        )
        value = jnp.where(lane < 3 * taps, value, jnp.where(lane < 32, rest, 0.0))
        win_a[base : base + CELLS, taps * C :] = value.astype(BF16)

    def work(step, carry):
        slots_at = [step * GROUP + part for part in range(GROUP)]
        real = [slot < count for slot in slots_at]
        used = [jnp.minimum(slot, count - 1) for slot in slots_at]
        for part in range(GROUP):
            @pl.when(real[part])
            def _(part=part):
                block_copy(used[part])[0].wait()

        rows = [slice(part * CELLS, (part + 1) * CELLS) for part in range(GROUP)]

        def first_layer(part):
            return jnp.dot(win_a[rows[part]], weight_a[...], preferred_element_type=F32)

        def activate(part, pre_a):
            gate = sigmoid(pre_a)
            act[rows[part]] = (pre_a * gate).astype(BF16)
            slope[rows[part]] = gate * (1.0 + pre_a * (1.0 - gate))

        def second_layer(part):
            return jnp.dot(act[rows[part]], weight_b[...], preferred_element_type=F32)

        def finish(part, product):
            columns = []
            for shift in range(3):
                tap = [product[:, (3 * r + shift) * C : (3 * r + shift + 1) * C] for r in range(3)]
                columns.append(from_previous_row(tap[0]) + tap[1] + from_next_row(tap[2]))
            pre_b = (
                ends[0:1]
                + from_previous_column(columns[0], cell_col)
                + columns[1]
                + from_next_column(columns[2], cell_col)
            )
            gate = sigmoid(pre_b)
            final = jnp.sum(pre_b * gate * ends[1:2], axis=1, keepdims=True)
            residual = final - aim[rows[part]]
            device, inner = fields(used[part])
            weight = jnp.where(real[part], ints[device, inner * FIELDS + 4], 0.0)
            loss = weight * jnp.sum(residual * residual) * (1.0 / (CELLS * C))
            spot = jnp.logical_and(loss_row == device, loss_lane == inner)
            loss_out[...] += jnp.where(spot, loss, 0.0)
            factor = (2.0 / CELLS) * weight * residual
            grad_pre_b = factor * ends[1:2] * (gate * (1.0 + pre_b * (1.0 - gate)))
            base = part * CELLS
            for shift, value in enumerate(
                (
                    from_next_column(grad_pre_b, cell_col),
                    grad_pre_b,
                    from_previous_column(grad_pre_b, cell_col),
                )
            ):
                value = value.astype(BF16)
                for shift_row in range(3):
                    lanes = pl.ds((3 * shift_row + shift) * C, C)
                    if shift_row == 0:
                        win_g[base : base + CELLS - P_SIZE, lanes] = value[P_SIZE:]
                    elif shift_row == 1:
                        win_g[base : base + CELLS, lanes] = value
                    else:
                        win_g[base + P_SIZE : base + CELLS, lanes] = value[: CELLS - P_SIZE]

        def hidden(part):
            return jnp.dot(win_g[rows[part]], weight_back[...], preferred_element_type=F32)

        def turn_back(part, grad_hidden):
            return (grad_hidden * slope[rows[part]]).astype(BF16)

        prepare(0, used[0])
        pre_0 = first_layer(0)
        prepare(1, used[1])
        pre_1 = first_layer(1)
        activate(0, pre_0)
        product_0 = second_layer(0)
        activate(1, pre_1)
        product_1 = second_layer(1)
        finish(0, product_0)
        hidden_0 = hidden(0)
        finish(1, product_1)
        hidden_1 = hidden(1)
        back_0 = turn_back(0, hidden_0)
        started = step > 0
        over_cells = (((0,), (0,)), ((), ()))
        grad_b[...] = jnp.where(started, grad_b[...], 0.0) + lax.dot_general(
            act[...], win_g[...], over_cells, preferred_element_type=F32
        )
        grad_pre_a = jnp.concatenate([back_0, turn_back(1, hidden_1)], axis=0)
        grad_a[...] = jnp.where(started, grad_a[...], 0.0) + lax.dot_general(
            grad_pre_a, win_a[:, : taps * C], over_cells, preferred_element_type=F32
        )
        return carry

    lax.fori_loop(0, lax.div(count + GROUP - 1, GROUP), work, 0)

    chunk = HID // devices
    for pair in range(devices // 2):
        for at, grad in ((0, grad_a), (taps * C, grad_b)):
            lanes = pl.ds(at, taps * C)
            even = grad[2 * pair * chunk : (2 * pair + 1) * chunk]
            odd = grad[(2 * pair + 1) * chunk : (2 * pair + 2) * chunk]
            first = my_core == 0
            keep_out[pair, :, lanes] = jnp.where(first, even, odd)
            send_out[pair, :, lanes] = jnp.where(first, odd, even).astype(BF16)


def halve_kernel(fan, count, step, keep, *refs):
    received, outs = refs[:count], refs[count:]
    index = lax.axis_index("tile") * lax.axis_size("dp") + lax.axis_index("dp")
    mine = lax.rem(lax.div(index, step), fan)
    for peer in range(fan):
        low = jnp.bitwise_xor(mine, peer)
        for high_part in range(keep.shape[0] // fan):
            at = high_part * fan + low
            total = keep[at]
            for other in received:
                total = total + other[at].astype(F32)
            outs[peer][high_part] = total.astype(outs[peer].dtype)


def finish_kernel(npatch, keep, losses, *refs):
    received, (grad, payload) = refs[:-2], refs[-2:]
    total = keep[0]
    for other in received:
        total = total + other[0].astype(F32)
    grad[...] = total
    half = total.shape[1] // 2
    lane = lax.broadcasted_iota(jnp.int32, losses.shape, 1)
    square_a = jnp.sum(total[:, :half] * total[:, :half])
    square_b = jnp.sum(total[:, half:] * total[:, half:])
    value = jnp.where(lane == npatch, square_a, losses[...])
    payload[:, 0, :] = jnp.where(lane == npatch + 1, square_b, value)


def scale_kernel(npatch, entries, grad, payload, losses, upd_a, upd_b):
    total = jnp.sum(payload[:, 0, :], axis=0, keepdims=True)
    lane = lax.broadcasted_iota(jnp.int32, total.shape, 1)
    for patch in range(npatch):
        losses[patch] = jnp.sum(jnp.where(lane == patch, total, 0.0))
    half = grad.shape[1] // 2
    for part, out in enumerate((upd_a, upd_b)):
        square = jnp.sum(jnp.where(lane == npatch + part, total, 0.0), axis=1, keepdims=True)
        out[...] = grad[:, part * half : (part + 1) * half] / jnp.sqrt(square / entries + EPSILON)


def local(
    features,
    target_field,
    owner_tile,
    row_offset,
    column_start,
    noise_level,
    icing_count,
    noise_draw,
    w_a,
    w_u,
    b_a,
    e_a,
    w_b,
    b_b,
    w_o,
):
    tile_count, dp_count = lax.axis_size("tile"), lax.axis_size("dp")
    devices = tile_count * dp_count
    npatch = owner_tile.shape[0]
    slots = max(2, 2 * npatch // tile_count) * devices // dp_count
    chunk = HID // devices
    width = 2 * 9 * C
    in_hbm = pl.BlockSpec(memory_space=pltpu.HBM)
    stay = functools.partial(pltpu.with_memory_space_constraint, memory_space=pltpu.HBM)
    in_vmem = pl.BlockSpec(memory_space=pltpu.VMEM)
    in_smem = pl.BlockSpec(memory_space=pltpu.SMEM)

    def room(mebibytes):
        return pltpu.CompilerParams(vmem_limit_bytes=mebibytes * 1024 * 1024)

    line = pl.pallas_call(
        pack_kernel,
        out_shape=jax.ShapeDtypeStruct((devices, 1, npatch * CELLS + C), F32),
        in_specs=[in_hbm] * 6,
        out_specs=in_vmem,
        scratch_shapes=[
            *[pltpu.SMEM((npatch,), jnp.int32)] * 5,
            pltpu.VMEM(noise_draw.shape, F32),
            pltpu.SemaphoreType.DMA((6,)),
        ],
        compiler_params=room(4),
        name="pack",
    )(
        *map(stay, (owner_tile.reshape(-1), row_offset, column_start, noise_level, icing_count, noise_draw))
    )
    table = lax.all_to_all(line, AXES, split_axis=0, concat_axis=0, tiled=True)

    weights = pl.pallas_call(
        weights_kernel,
        out_shape=(
            pltpu.HBM((10 * C, HID), BF16),
            pltpu.HBM((HID, 9 * C), BF16),
            pltpu.HBM((9 * C, HID), BF16),
            pltpu.HBM((2, C), F32),
            pltpu.HBM(target_field.shape, F32),
        ),
        in_specs=[in_hbm] * 8,
        out_specs=(in_vmem,) * 5,
        scratch_shapes=[
            pltpu.VMEM((9, HID), F32),
            pltpu.VMEM((1, HID), F32),
            pltpu.VMEM((1, HID), F32),
            pltpu.VMEM((C, HID), F32),
            pltpu.VMEM(target_field.shape, BF16),
            pltpu.SemaphoreType.DMA((16,)),
        ],
        compiler_params=room(8),
        name="weights",
    )(
        stay(w_a),
        stay(w_u),
        stay(b_a.reshape(1, -1)),
        stay(e_a.reshape(1, -1)),
        stay(w_b),
        stay(b_b.reshape(1, -1)),
        stay(w_o.reshape(1, -1)),
        stay(target_field),
    )
    weight_a, weight_b, weight_back, ends, target32 = weights

    keep, send, losses = pl.pallas_call(
        functools.partial(train_kernel, dp_count, npatch),
        out_shape=(
            pltpu.VMEM((devices // 2, chunk, width), F32),
            pltpu.VMEM((devices // 2, chunk, width), BF16),
            pltpu.VMEM((devices, C), F32),
        ),
        in_specs=[in_hbm, in_vmem] + [in_hbm] * 6,
        out_specs=(in_vmem, in_vmem, in_vmem),
        scratch_shapes=[
            pltpu.SMEM((devices, C), F32),
            pltpu.SMEM((slots + 1,), jnp.int32),
            pltpu.VMEM((slots, P_SIZE, SPAN, C), BF16),
            pltpu.VMEM(target_field.shape, F32),
            pltpu.VMEM((10 * C, HID), BF16),
            pltpu.VMEM((HID, 9 * C), BF16),
            pltpu.VMEM((9 * C, HID), BF16),
            pltpu.VMEM((2, C), F32),
            pltpu.VMEM((GROUP * CELLS, 10 * C), BF16),
            pltpu.VMEM((GROUP * CELLS, HID), BF16),
            pltpu.VMEM((GROUP * CELLS, 9 * C), BF16),
            pltpu.VMEM((GROUP * CELLS, HID), F32),
            pltpu.VMEM((GROUP * CELLS, C), F32),
            pltpu.VMEM((HID, 9 * C), F32),
            pltpu.VMEM((HID, 9 * C), F32),
            pltpu.SemaphoreType.DMA,
            pltpu.SemaphoreType.DMA((5,)),
            pltpu.SemaphoreType.DMA((slots,)),
        ],
        compiler_params=room(32),
        name="train",
    )(table, table, *map(stay, (features, target32, weight_a, weight_b, weight_back, ends)))

    def exchange(array, distance):
        return lax.ppermute(array, AXES, [(i, i ^ distance) for i in range(devices)])

    received = [exchange(send, 1)]
    step = 2
    while step < devices:
        fan = min(8, devices // step)
        part = (keep.shape[0] // fan, chunk, width)
        outs = pl.pallas_call(
            functools.partial(halve_kernel, fan, len(received), step),
            out_shape=(
                pltpu.VMEM(part, F32),
                *[pltpu.VMEM(part, BF16) for _ in range(fan - 1)],
            ),
            in_specs=[in_vmem] * (1 + len(received)),
            out_specs=(in_vmem,) * fan,
            compiler_params=room(8),
            name=f"halve_{step}",
        )(keep, *received)
        keep = outs[0]
        received = [exchange(outs[peer], peer * step) for peer in range(1, fan)]
        step *= fan

    grad, payload = pl.pallas_call(
        functools.partial(finish_kernel, npatch),
        out_shape=(
            pltpu.VMEM((chunk, width), F32),
            pltpu.VMEM((devices, 1, C), F32),
        ),
        in_specs=[in_vmem] * (2 + len(received)),
        out_specs=(in_vmem, in_vmem),
        compiler_params=room(4),
        name="finish",
    )(keep, losses, *received)
    payload = lax.all_to_all(payload, AXES, split_axis=0, concat_axis=0, tiled=True)
    out = jax.ShapeDtypeStruct((chunk, width // 2), F32)
    sums, upd_a, upd_b = pl.pallas_call(
        functools.partial(scale_kernel, npatch, HID * 9 * C),
        out_shape=(jax.ShapeDtypeStruct((npatch,), F32), out, out),
        in_specs=[in_vmem, in_vmem],
        out_specs=(in_smem, in_vmem, in_vmem),
        compiler_params=room(4),
        name="scale",
    )(grad, payload)
    return sums, upd_a, upd_b


def solution(mesh):
    both = P(AXES)
    return jax.shard_map(
        local,
        mesh=mesh,
        in_specs=(
            P("tile", None, None),
            P("tile", None),
            P(AXES, None),
            both,
            both,
            both,
            both,
            P(AXES, None, None),
            P(),
            P(),
            P(),
            P(),
            P(),
            P(),
            P(),
        ),
        out_specs=(both, P(AXES, None), P(AXES, None)),
        check_vma=False,
    )
```

```python
import functools
import math

import jax
import jax.numpy as jnp
from jax import lax
from jax.experimental import pallas as pl
from jax.experimental.pallas import tpu as pltpu
from jax.sharding import PartitionSpec as P

C = 128
HID = 512
P_SIZE = 16
LEVELS = 32
CELLS = P_SIZE * P_SIZE
SPAN = 32
FIELDS = 8
GROUP = 2

SIGMA_LOW = 0.02
SIGMA_HIGH = 80.0
SIGMA_DATA = 0.5
EPSILON = 1e-06
AXES = ("tile", "dp")
BF16 = jnp.bfloat16
F32 = jnp.float32


def sigmoid(values):
    return 0.5 * jnp.tanh(0.5 * values) + 0.5


def from_previous_column(x, col):
    return jnp.where(col == 0, 0.0, pltpu.roll(x, 1, 0))


def from_next_column(x, col):
    return jnp.where(col == P_SIZE - 1, 0.0, pltpu.roll(x, x.shape[0] - 1, 0))


def from_previous_row(x):
    zero = jnp.zeros((P_SIZE, x.shape[1]), x.dtype)
    parts = []
    for at in range(0, x.shape[0], CELLS):
        parts += [zero, x[at : at + CELLS - P_SIZE]]
    return jnp.concatenate(parts, axis=0)


def from_next_row(x):
    zero = jnp.zeros((P_SIZE, x.shape[1]), x.dtype)
    parts = []
    for at in range(0, x.shape[0], CELLS):
        parts += [x[at + P_SIZE : at + CELLS], zero]
    return jnp.concatenate(parts, axis=0)


def high(value):
    return value.astype(BF16).astype(F32)


def store_window(ref, base, tap, rows):
    lanes = pl.ds(tap * C, C)
    shift = tap // 3
    if shift == 0:
        ref[base + P_SIZE : base + CELLS, lanes] = rows[: CELLS - P_SIZE]
    elif shift == 1:
        ref[base : base + CELLS, lanes] = rows
    else:
        ref[base : base + CELLS - P_SIZE, lanes] = rows[P_SIZE:]


def pack_kernel(*refs):
    sources, line, scratch, sems = refs[:6], refs[6], refs[7:13], refs[13]
    copies = [
        pltpu.make_async_copy(src, dst, sems.at[at]) for at, (src, dst) in enumerate(zip(sources, scratch))
    ]
    for copy in copies:
        copy.start()
    *integers, drawn = scratch
    npatch = drawn.shape[0]
    lane = lax.broadcasted_iota(jnp.int32, (1, C), 1)
    numbers = jnp.zeros((1, C), jnp.int32)
    for copy in copies:
        copy.wait()
    for patch in range(npatch):
        for at, ref in enumerate(integers):
            numbers = jnp.where(lane == patch * FIELDS + at, ref[patch], numbers)
    shape = (line.shape[0], 1, C)
    line[:, :, npatch * CELLS :] = jnp.broadcast_to(numbers.astype(F32)[None], shape)
    rows = C // P_SIZE
    mine = lax.broadcasted_iota(jnp.int32, (rows, C), 0)
    here = lax.broadcasted_iota(jnp.int32, (rows, C), 1) // P_SIZE == mine
    for patch in range(npatch):
        for at in range(0, P_SIZE, rows):
            part = drawn[patch, at : at + rows, :]
            spread = jnp.concatenate([part] * rows, axis=1)
            flat = jnp.sum(jnp.where(here, spread, 0.0), axis=0, keepdims=True)
            start = patch * CELLS + at * P_SIZE
            line[:, :, start : start + C] = jnp.broadcast_to(flat[None], shape)


def weights_kernel(
    w_a, w_u, b_a, e_a, w_b, b_b, w_o, target,
    weight_a, weight_b, weight_back, ends, target32,
    small_u, small_b, small_e, extra32, field, sems,
):
    taps = 9
    copies = [
        pltpu.make_async_copy(w_b.at[pl.ds(tap * HID, HID)], weight_b.at[:, pl.ds(tap * C, C)], sems.at[tap])
        for tap in range(taps)
    ]
    places = (
        (w_a, weight_a.at[pl.ds(0, taps * C)]),
        (w_u, small_u),
        (b_a, small_b),
        (e_a, small_e),
        (b_b, ends.at[pl.ds(0, 1)]),
        (w_o, ends.at[pl.ds(1, 1)]),
        (target, field),
    )
    smalls = [pltpu.make_async_copy(src, dst, sems.at[taps + at]) for at, (src, dst) in enumerate(places)]
    for copy in smalls + copies:
        copy.start()
    for copy in smalls[1:]:
        copy.wait()
    target32[...] = field[...].astype(F32)
    extra32[...] = jnp.zeros_like(extra32)
    w_u_value, b_a_value, e_a_value = small_u[...], small_b[...], small_e[...]
    extra32[0:taps] = high(w_u_value)
    extra32[taps : 2 * taps] = w_u_value - high(w_u_value)
    extra32[2 * taps : 3 * taps] = high(w_u_value)
    extra32[27:28] = high(b_a_value)
    extra32[28:29] = b_a_value - high(b_a_value)
    extra32[29:30] = high(e_a_value)
    extra32[30:31] = e_a_value - high(e_a_value)
    extra32[31:32] = high(e_a_value)
    weight_a[taps * C :] = extra32[...].astype(BF16)
    for tap, copy in enumerate(copies):
        copy.wait()
        weight_back[tap * C : (tap + 1) * C, :] = weight_b[:, tap * C : (tap + 1) * C].T
    smalls[0].wait()


def train_kernel(
    dp_count,
    npatch,
    table_hbm,
    table,
    features,
    target32_hbm,
    weight_a_hbm,
    weight_b_hbm,
    weight_back_hbm,
    ends_hbm,
    keep_out,
    send_out,
    loss_out,
    ints,
    chosen,
    blocks,
    target32,
    weight_a,
    weight_b,
    weight_back,
    ends,
    win_a,
    act,
    win_g,
    slope,
    aim,
    grad_a,
    grad_b,
    tails,
    int_sem,
    weight_sems,
    block_sems,
):
    devices = table.shape[0]
    slots = blocks.shape[0]
    taps = 9
    my_tile, my_dp = lax.axis_index("tile"), lax.axis_index("dp")
    my_core = lax.rem(my_tile * dp_count + my_dp, 2)

    copy_ints = pltpu.make_async_copy(table_hbm.at[:, 0, pl.ds(npatch * CELLS, C)], ints, int_sem)
    copy_ints.start()
    operands = (
        (target32_hbm, target32),
        (ends_hbm, ends),
        (weight_a_hbm, weight_a),
        (weight_b_hbm, weight_b),
        (weight_back_hbm, weight_back),
    )
    copies = [pltpu.make_async_copy(src, dst, weight_sems.at[at]) for at, (src, dst) in enumerate(operands)]
    for copy in copies:
        copy.start()
    copy_ints.wait()

    tile_name = my_tile.astype(F32)

    def choose(device, carry):
        turn, place_at = carry
        for patch in range(npatch):
            owned = ints[device, patch * FIELDS] == tile_name
            mine = jnp.logical_and(owned, turn == my_dp)
            chosen[jnp.where(mine, place_at, slots)] = device * npatch + patch
            place_at = jnp.where(mine, place_at + 1, place_at)
            following = jnp.where(turn == dp_count - 1, 0, turn + 1)
            turn = jnp.where(owned, following, turn)
        return turn, place_at


    def fields(slot):
        patch = chosen[slot]
        device = lax.div(patch, npatch)
        inner = lax.rem(patch, npatch)
        return device, inner

    def block_copy(slot):
        device, inner = fields(slot)
        row = ints[device, inner * FIELDS + 1].astype(jnp.int32)
        column = ints[device, inner * FIELDS + 2].astype(jnp.int32)
        most = (features.shape[1] - SPAN) // 16
        start = jnp.minimum(lax.shift_right_logical(column, 4), most) * 16
        start = pl.multiple_of(start, 16)
        copy = pltpu.make_async_copy(
            features.at[pl.ds(row, P_SIZE), pl.ds(start, SPAN)],
            blocks.at[slot],
            block_sems.at[slot],
        )
        return copy, row, column, column - start

    def start_block(slot, carry):
        block_copy(slot)[0].start()
        return carry

    turn, count = jnp.int32(0), jnp.int32(0)
    stops = [0, devices // 4, devices // 2, devices]
    for begin, end in zip(stops, stops[1:]):
        known = count
        turn, count = lax.fori_loop(begin, end, choose, (turn, known))
        lax.fori_loop(known, count, start_block, 0)

    @pl.when(count == 0)
    def _():
        grad_a[...] = jnp.zeros_like(grad_a)
        grad_b[...] = jnp.zeros_like(grad_b)
        tails[...] = jnp.zeros_like(tails)

    loss_out[...] = jnp.zeros_like(loss_out)
    edge = jnp.zeros((P_SIZE, 3 * C), BF16)
    for part in range(GROUP):
        first, last = part * CELLS, (part + 1) * CELLS - P_SIZE
        win_a[first : first + P_SIZE, : 3 * C] = edge
        win_a[last : last + P_SIZE, 6 * C : 9 * C] = edge
        win_g[last : last + P_SIZE, : 3 * C] = edge
        win_g[first : first + P_SIZE, 6 * C : 9 * C] = edge

    for copy in copies:
        copy.wait()

    cell_col = lax.broadcasted_iota(jnp.int32, (CELLS, C), 0) & (P_SIZE - 1)
    lane = lax.broadcasted_iota(jnp.int32, (CELLS, C), 1)
    lane_tap = lax.rem(lane, taps)
    lane_row, lane_col = lax.div(lane_tap, 3), lax.rem(lane_tap, 3)
    pick_shape = (P_SIZE, P_SIZE, C)
    tile_line = lax.broadcasted_iota(jnp.int32, (P_SIZE * SPAN // 8, 8, C), 1)
    pick_row = lax.broadcasted_iota(jnp.int32, pick_shape, 0) & 7
    pick_col = lax.broadcasted_iota(jnp.int32, pick_shape, 1)
    pick_lane = lax.broadcasted_iota(jnp.int32, pick_shape, 2)
    noise_pick = pick_lane == pick_row * P_SIZE + pick_col
    field_shape = (P_SIZE, P_SIZE, target32.shape[1])
    field_col = lax.broadcasted_iota(jnp.int32, field_shape, 1)
    field_lane = lax.broadcasted_iota(jnp.int32, field_shape, 2)
    loss_row = lax.broadcasted_iota(jnp.int32, loss_out.shape, 0)
    loss_lane = lax.broadcasted_iota(jnp.int32, loss_out.shape, 1)
    log_step = (math.log(SIGMA_HIGH) - math.log(SIGMA_LOW)) / (LEVELS - 1)

    def prepare(part, slot):
        base = part * CELLS
        copy, row, _, offset = block_copy(slot)
        device, inner = fields(slot)
        column = ints[device, inner * FIELDS + 2].astype(jnp.int32)
        level = ints[device, inner * FIELDS + 3]

        tiles = blocks[slot].astype(F32).reshape(P_SIZE * SPAN // 8, 8, C)
        within = offset & 7
        turned = pltpu.roll(tiles, (8 - within) & 7, 1)
        after = jnp.concatenate([turned[1:], turned[:1]], axis=0)
        tiles = jnp.where(tile_line + within < 8, turned, after).reshape(P_SIZE, SPAN // 8, 8, C)
        whole_tiles = lax.shift_right_logical(offset, 3)
        block = jnp.where(
            whole_tiles == 0,
            tiles[:, 0:2],
            jnp.where(whole_tiles == 1, tiles[:, 1:3], tiles[:, 2:4]),
        ).reshape(CELLS, C)
        for shift, value in enumerate(
            (from_previous_column(block, cell_col), block, from_next_column(block, cell_col))
        ):
            value = value.astype(BF16)
            for shift_row in range(3):
                store_window(win_a, base, 3 * shift_row + shift, value)

        log_sigma = math.log(SIGMA_LOW) + jnp.full((1, 1), level) * log_step
        sigma = jnp.exp(log_sigma)
        variance = sigma * sigma + SIGMA_DATA * SIGMA_DATA
        scale_in = 1.0 / jnp.sqrt(variance)
        embed = jnp.log(sigma) / 4.0

        tile_rows = target32.shape[0]
        lines = pltpu.roll(target32[...], lax.rem(tile_rows - row, tile_rows), 0)[:P_SIZE]
        clean = jnp.sum(
            jnp.where(field_lane == column + field_col, lines[:, None, :], 0.0),
            axis=2,
            keepdims=True,
        )
        at = pl.multiple_of(inner * CELLS, C)
        first = table[device, :, pl.ds(at, C)]
        second = table[device, :, pl.ds(pl.multiple_of(at + C, C), C)]
        half = (P_SIZE // 2, P_SIZE, C)
        drawn = jnp.concatenate(
            [jnp.broadcast_to(first[None], half), jnp.broadcast_to(second[None], half)], axis=0
        )
        noise = jnp.sum(jnp.where(noise_pick, drawn, 0.0), axis=2, keepdims=True)
        clean = jnp.broadcast_to(clean, pick_shape).reshape(CELLS, C)
        noise = jnp.broadcast_to(noise, pick_shape).reshape(CELLS, C)
        scaled = scale_in * (clean + sigma * noise)
        aim[base : base + CELLS] = scale_in * (2.0 * sigma * clean - 0.5 * noise)

        rows = jnp.where(
            lane_row == 0,
            from_previous_row(scaled),
            jnp.where(lane_row == 2, from_next_row(scaled), scaled),
        )
        moved = jnp.where(
            lane_col == 0,
            from_previous_column(rows, cell_col),
            jnp.where(lane_col == 2, from_next_column(rows, cell_col), rows),
        )
        moved_high = high(moved)
        value = jnp.where(lane < 2 * taps, moved_high, moved - moved_high)
        embed_high = high(embed)
        rest = jnp.where(
            lane < 29, 1.0, jnp.where(lane < 31, embed_high, embed - embed_high)
        )
        value = jnp.where(lane < 3 * taps, value, jnp.where(lane < 32, rest, 0.0))
        win_a[base : base + CELLS, taps * C :] = value.astype(BF16)

    def work(step, carry):
        slots_at = [step * GROUP + part for part in range(GROUP)]
        real = [slot < count for slot in slots_at]
        used = [jnp.minimum(slot, count - 1) for slot in slots_at]
        for part in range(GROUP):
            @pl.when(real[part])
            def _(part=part):
                block_copy(used[part])[0].wait()

        rows = [slice(part * CELLS, (part + 1) * CELLS) for part in range(GROUP)]

        def first_layer(part):
            return jnp.dot(win_a[rows[part]], weight_a[...], preferred_element_type=F32)

        def activate(part, pre_a):
            gate = sigmoid(pre_a)
            act[rows[part]] = (pre_a * gate).astype(BF16)
            slope[rows[part]] = gate * (1.0 + pre_a * (1.0 - gate))

        def second_layer(part):
            return jnp.dot(act[rows[part]], weight_b[...], preferred_element_type=F32)

        def finish(part, product):
            columns = []
            for shift in range(3):
                tap = [product[:, (3 * r + shift) * C : (3 * r + shift + 1) * C] for r in range(3)]
                columns.append(from_previous_row(tap[0]) + tap[1] + from_next_row(tap[2]))
            pre_b = (
                ends[0:1]
                + from_previous_column(columns[0], cell_col)
                + columns[1]
                + from_next_column(columns[2], cell_col)
            )
            gate = sigmoid(pre_b)
            final = jnp.sum(pre_b * gate * ends[1:2], axis=1, keepdims=True)
            residual = final - aim[rows[part]]
            device, inner = fields(used[part])
            weight = jnp.where(real[part], ints[device, inner * FIELDS + 4], 0.0)
            loss = weight * jnp.sum(residual * residual) * (1.0 / (CELLS * C))
            spot = jnp.logical_and(loss_row == device, loss_lane == inner)
            loss_out[...] += jnp.where(spot, loss, 0.0)
            factor = (2.0 / CELLS) * weight * residual
            grad_pre_b = factor * ends[1:2] * (gate * (1.0 + pre_b * (1.0 - gate)))
            base = part * CELLS
            for shift, value in enumerate(
                (
                    from_next_column(grad_pre_b, cell_col),
                    grad_pre_b,
                    from_previous_column(grad_pre_b, cell_col),
                )
            ):
                value = value.astype(BF16)
                for shift_row in range(3):
                    lanes = pl.ds((3 * shift_row + shift) * C, C)
                    if shift_row == 0:
                        win_g[base : base + CELLS - P_SIZE, lanes] = value[P_SIZE:]
                    elif shift_row == 1:
                        win_g[base : base + CELLS, lanes] = value
                    else:
                        win_g[base + P_SIZE : base + CELLS, lanes] = value[: CELLS - P_SIZE]

        def hidden(part):
            return jnp.dot(win_g[rows[part]], weight_back[...], preferred_element_type=F32)

        def turn_back(part, grad_hidden):
            return (grad_hidden * slope[rows[part]]).astype(BF16)

        prepare(0, used[0])
        pre_0 = first_layer(0)
        prepare(1, used[1])
        pre_1 = first_layer(1)
        activate(0, pre_0)
        product_0 = second_layer(0)
        activate(1, pre_1)
        product_1 = second_layer(1)
        finish(0, product_0)
        hidden_0 = hidden(0)
        finish(1, product_1)
        hidden_1 = hidden(1)
        back_0 = turn_back(0, hidden_0)
        started = step > 0
        over_cells = (((0,), (0,)), ((), ()))

        def add(at, grad, rows_of, columns_of):
            wide = columns_of[:, : 8 * C]
            grad[:, : 8 * C] = jnp.where(started, grad[:, : 8 * C], 0.0) + lax.dot_general(
                rows_of, wide, over_cells, preferred_element_type=F32
            )
            last = columns_of[:, 8 * C : 9 * C]
            tails[at] = jnp.where(started, tails[at], 0.0) + lax.dot_general(
                last, rows_of, over_cells, preferred_element_type=F32
            )

        add(1, grad_b, act[...], win_g)
        add(0, grad_a, jnp.concatenate([back_0, turn_back(1, hidden_1)], axis=0), win_a)
        return carry

    lax.fori_loop(0, lax.div(count + GROUP - 1, GROUP), work, 0)
    grad_a[:, 8 * C :] = tails[0].T
    grad_b[:, 8 * C :] = tails[1].T

    chunk = HID // devices
    for pair in range(devices // 2):
        for at, grad in ((0, grad_a), (taps * C, grad_b)):
            lanes = pl.ds(at, taps * C)
            even = grad[2 * pair * chunk : (2 * pair + 1) * chunk]
            odd = grad[(2 * pair + 1) * chunk : (2 * pair + 2) * chunk]
            first = my_core == 0
            keep_out[pair, :, lanes] = jnp.where(first, even, odd)
            send_out[pair, :, lanes] = jnp.where(first, odd, even).astype(BF16)


def halve_kernel(fan, count, step, keep, *refs):
    received, outs = refs[:count], refs[count:]
    index = lax.axis_index("tile") * lax.axis_size("dp") + lax.axis_index("dp")
    mine = lax.rem(lax.div(index, step), fan)
    for peer in range(fan):
        low = jnp.bitwise_xor(mine, peer)
        for high_part in range(keep.shape[0] // fan):
            at = high_part * fan + low
            total = keep[at]
            for other in received:
                total = total + other[at].astype(F32)
            outs[peer][high_part] = total.astype(outs[peer].dtype)


def finish_kernel(npatch, keep, losses, *refs):
    received, (grad, payload) = refs[:-2], refs[-2:]
    total = keep[0]
    for other in received:
        total = total + other[0].astype(F32)
    grad[...] = total
    half = total.shape[1] // 2
    lane = lax.broadcasted_iota(jnp.int32, losses.shape, 1)
    square_a = jnp.sum(total[:, :half] * total[:, :half])
    square_b = jnp.sum(total[:, half:] * total[:, half:])
    value = jnp.where(lane == npatch, square_a, losses[...])
    payload[:, 0, :] = jnp.where(lane == npatch + 1, square_b, value)


def scale_kernel(npatch, entries, grad, payload, losses, upd_a, upd_b):
    total = jnp.sum(payload[:, 0, :], axis=0, keepdims=True)
    lane = lax.broadcasted_iota(jnp.int32, total.shape, 1)
    for patch in range(npatch):
        losses[patch] = jnp.sum(jnp.where(lane == patch, total, 0.0))
    half = grad.shape[1] // 2
    for part, out in enumerate((upd_a, upd_b)):
        square = jnp.sum(jnp.where(lane == npatch + part, total, 0.0), axis=1, keepdims=True)
        out[...] = grad[:, part * half : (part + 1) * half] / jnp.sqrt(square / entries + EPSILON)


def local(
    features,
    target_field,
    owner_tile,
    row_offset,
    column_start,
    noise_level,
    icing_count,
    noise_draw,
    w_a,
    w_u,
    b_a,
    e_a,
    w_b,
    b_b,
    w_o,
):
    tile_count, dp_count = lax.axis_size("tile"), lax.axis_size("dp")
    devices = tile_count * dp_count
    npatch = owner_tile.shape[0]
    slots = max(2, 2 * npatch // tile_count) * devices // dp_count
    chunk = HID // devices
    width = 2 * 9 * C
    in_hbm = pl.BlockSpec(memory_space=pltpu.HBM)
    stay = functools.partial(pltpu.with_memory_space_constraint, memory_space=pltpu.HBM)
    in_vmem = pl.BlockSpec(memory_space=pltpu.VMEM)
    in_smem = pl.BlockSpec(memory_space=pltpu.SMEM)

    def room(mebibytes):
        return pltpu.CompilerParams(vmem_limit_bytes=mebibytes * 1024 * 1024)

    line = pl.pallas_call(
        pack_kernel,
        out_shape=jax.ShapeDtypeStruct((devices, 1, npatch * CELLS + C), F32),
        in_specs=[in_hbm] * 6,
        out_specs=in_vmem,
        scratch_shapes=[
            *[pltpu.SMEM((npatch,), jnp.int32)] * 5,
            pltpu.VMEM(noise_draw.shape, F32),
            pltpu.SemaphoreType.DMA((6,)),
        ],
        compiler_params=room(4),
        name="pack",
    )(
        *map(stay, (owner_tile.reshape(-1), row_offset, column_start, noise_level, icing_count, noise_draw))
    )
    table = lax.all_to_all(line, AXES, split_axis=0, concat_axis=0, tiled=True)

    weights = pl.pallas_call(
        weights_kernel,
        out_shape=(
            pltpu.HBM((10 * C, HID), BF16),
            pltpu.HBM((HID, 9 * C), BF16),
            pltpu.HBM((9 * C, HID), BF16),
            pltpu.HBM((2, C), F32),
            pltpu.HBM(target_field.shape, F32),
        ),
        in_specs=[in_hbm] * 8,
        out_specs=(in_vmem,) * 5,
        scratch_shapes=[
            pltpu.VMEM((9, HID), F32),
            pltpu.VMEM((1, HID), F32),
            pltpu.VMEM((1, HID), F32),
            pltpu.VMEM((C, HID), F32),
            pltpu.VMEM(target_field.shape, BF16),
            pltpu.SemaphoreType.DMA((16,)),
        ],
        compiler_params=room(8),
        name="weights",
    )(
        stay(w_a),
        stay(w_u),
        stay(b_a.reshape(1, -1)),
        stay(e_a.reshape(1, -1)),
        stay(w_b),
        stay(b_b.reshape(1, -1)),
        stay(w_o.reshape(1, -1)),
        stay(target_field),
    )
    weight_a, weight_b, weight_back, ends, target32 = weights

    keep, send, losses = pl.pallas_call(
        functools.partial(train_kernel, dp_count, npatch),
        out_shape=(
            pltpu.VMEM((devices // 2, chunk, width), F32),
            pltpu.VMEM((devices // 2, chunk, width), BF16),
            pltpu.VMEM((devices, C), F32),
        ),
        in_specs=[in_hbm, in_vmem] + [in_hbm] * 6,
        out_specs=(in_vmem, in_vmem, in_vmem),
        scratch_shapes=[
            pltpu.SMEM((devices, C), F32),
            pltpu.SMEM((slots + 1,), jnp.int32),
            pltpu.VMEM((slots, P_SIZE, SPAN, C), BF16),
            pltpu.VMEM(target_field.shape, F32),
            pltpu.VMEM((10 * C, HID), BF16),
            pltpu.VMEM((HID, 9 * C), BF16),
            pltpu.VMEM((9 * C, HID), BF16),
            pltpu.VMEM((2, C), F32),
            pltpu.VMEM((GROUP * CELLS, 10 * C), BF16),
            pltpu.VMEM((GROUP * CELLS, HID), BF16),
            pltpu.VMEM((GROUP * CELLS, 9 * C), BF16),
            pltpu.VMEM((GROUP * CELLS, HID), F32),
            pltpu.VMEM((GROUP * CELLS, C), F32),
            pltpu.VMEM((HID, 9 * C), F32),
            pltpu.VMEM((HID, 9 * C), F32),
            pltpu.VMEM((2, C, HID), F32),
            pltpu.SemaphoreType.DMA,
            pltpu.SemaphoreType.DMA((5,)),
            pltpu.SemaphoreType.DMA((slots,)),
        ],
        compiler_params=room(32),
        name="train",
    )(table, table, *map(stay, (features, target32, weight_a, weight_b, weight_back, ends)))

    def exchange(array, distance):
        return lax.ppermute(array, AXES, [(i, i ^ distance) for i in range(devices)])

    received = [exchange(send, 1)]
    step = 2
    while step < devices:
        fan = min(8, devices // step)
        part = (keep.shape[0] // fan, chunk, width)
        outs = pl.pallas_call(
            functools.partial(halve_kernel, fan, len(received), step),
            out_shape=(
                pltpu.VMEM(part, F32),
                *[pltpu.VMEM(part, BF16) for _ in range(fan - 1)],
            ),
            in_specs=[in_vmem] * (1 + len(received)),
            out_specs=(in_vmem,) * fan,
            compiler_params=room(8),
            name=f"halve_{step}",
        )(keep, *received)
        keep = outs[0]
        received = [exchange(outs[peer], peer * step) for peer in range(1, fan)]
        step *= fan

    grad, payload = pl.pallas_call(
        functools.partial(finish_kernel, npatch),
        out_shape=(
            pltpu.VMEM((chunk, width), F32),
            pltpu.VMEM((devices, 1, C), F32),
        ),
        in_specs=[in_vmem] * (2 + len(received)),
        out_specs=(in_vmem, in_vmem),
        compiler_params=room(4),
        name="finish",
    )(keep, losses, *received)
    payload = lax.all_to_all(payload, AXES, split_axis=0, concat_axis=0, tiled=True)
    out = jax.ShapeDtypeStruct((chunk, width // 2), F32)
    sums, upd_a, upd_b = pl.pallas_call(
        functools.partial(scale_kernel, npatch, HID * 9 * C),
        out_shape=(jax.ShapeDtypeStruct((npatch,), F32), out, out),
        in_specs=[in_vmem, in_vmem],
        out_specs=(in_smem, in_vmem, in_vmem),
        compiler_params=room(4),
        name="scale",
    )(grad, payload)
    return sums, upd_a, upd_b


def solution(mesh):
    both = P(AXES)
    return jax.shard_map(
        local,
        mesh=mesh,
        in_specs=(
            P("tile", None, None),
            P("tile", None),
            P(AXES, None),
            both,
            both,
            both,
            both,
            P(AXES, None, None),
            P(),
            P(),
            P(),
            P(),
            P(),
            P(),
            P(),
        ),
        out_specs=(both, P(AXES, None), P(AXES, None)),
        check_vma=False,
    )
```

```python
import functools
import math

import jax
import jax.numpy as jnp
from jax import lax
from jax.experimental import pallas as pl
from jax.experimental.pallas import tpu as pltpu
from jax.sharding import PartitionSpec as P

C = 128
HID = 512
P_SIZE = 16
LEVELS = 32
CELLS = P_SIZE * P_SIZE
SPAN = 32
FIELDS = 8
GROUP = 2

SIGMA_LOW = 0.02
SIGMA_HIGH = 80.0
SIGMA_DATA = 0.5
EPSILON = 1e-06
AXES = ("tile", "dp")
BF16 = jnp.bfloat16
F32 = jnp.float32


def sigmoid(values):
    return 0.5 * jnp.tanh(0.5 * values) + 0.5


def from_previous_column(x, col):
    return jnp.where(col == 0, 0.0, pltpu.roll(x, 1, 0))


def from_next_column(x, col):
    return jnp.where(col == P_SIZE - 1, 0.0, pltpu.roll(x, x.shape[0] - 1, 0))


def from_previous_row(x):
    zero = jnp.zeros((P_SIZE, x.shape[1]), x.dtype)
    parts = []
    for at in range(0, x.shape[0], CELLS):
        parts += [zero, x[at : at + CELLS - P_SIZE]]
    return jnp.concatenate(parts, axis=0)


def from_next_row(x):
    zero = jnp.zeros((P_SIZE, x.shape[1]), x.dtype)
    parts = []
    for at in range(0, x.shape[0], CELLS):
        parts += [x[at + P_SIZE : at + CELLS], zero]
    return jnp.concatenate(parts, axis=0)


def high(value):
    return value.astype(BF16).astype(F32)


def store_window(ref, base, tap, rows):
    lanes = pl.ds(tap * C, C)
    shift = tap // 3
    if shift == 0:
        ref[base + P_SIZE : base + CELLS, lanes] = rows[: CELLS - P_SIZE]
    elif shift == 1:
        ref[base : base + CELLS, lanes] = rows
    else:
        ref[base : base + CELLS - P_SIZE, lanes] = rows[P_SIZE:]


def pack_kernel(*refs):
    sources, line, scratch, sems = refs[:6], refs[6], refs[7:13], refs[13]
    copies = [
        pltpu.make_async_copy(src, dst, sems.at[at]) for at, (src, dst) in enumerate(zip(sources, scratch))
    ]
    for copy in copies:
        copy.start()
    *integers, drawn = scratch
    npatch = drawn.shape[0]
    lane = lax.broadcasted_iota(jnp.int32, (1, C), 1)
    numbers = jnp.zeros((1, C), jnp.int32)
    for copy in copies:
        copy.wait()
    for patch in range(npatch):
        for at, ref in enumerate(integers):
            numbers = jnp.where(lane == patch * FIELDS + at, ref[patch], numbers)
    shape = (line.shape[0], 1, C)
    line[:, :, npatch * CELLS :] = jnp.broadcast_to(numbers.astype(F32)[None], shape)
    rows = C // P_SIZE
    mine = lax.broadcasted_iota(jnp.int32, (rows, C), 0)
    here = lax.broadcasted_iota(jnp.int32, (rows, C), 1) // P_SIZE == mine
    for patch in range(npatch):
        for at in range(0, P_SIZE, rows):
            part = drawn[patch, at : at + rows, :]
            spread = jnp.concatenate([part] * rows, axis=1)
            flat = jnp.sum(jnp.where(here, spread, 0.0), axis=0, keepdims=True)
            start = patch * CELLS + at * P_SIZE
            line[:, :, start : start + C] = jnp.broadcast_to(flat[None], shape)


def weights_kernel(
    w_a, w_u, b_a, e_a, w_b, b_b, w_o, target,
    weight_a, weight_b, weight_back, ends, target32,
    small_u, small_b, small_e, extra32, field, sems,
):
    taps = 9
    copies = [
        pltpu.make_async_copy(w_b.at[pl.ds(tap * HID, HID)], weight_b.at[:, pl.ds(tap * C, C)], sems.at[tap])
        for tap in range(taps)
    ]
    places = (
        (w_a, weight_a.at[pl.ds(0, taps * C)]),
        (w_u, small_u),
        (b_a, small_b),
        (e_a, small_e),
        (b_b, ends.at[pl.ds(0, 1)]),
        (w_o, ends.at[pl.ds(1, 1)]),
        (target, field),
    )
    smalls = [pltpu.make_async_copy(src, dst, sems.at[taps + at]) for at, (src, dst) in enumerate(places)]
    for copy in smalls + copies:
        copy.start()
    for copy in smalls[1:]:
        copy.wait()
    target32[...] = field[...].astype(F32)
    extra32[...] = jnp.zeros_like(extra32)
    w_u_value, b_a_value, e_a_value = small_u[...], small_b[...], small_e[...]
    extra32[0:taps] = high(w_u_value)
    extra32[taps : 2 * taps] = w_u_value - high(w_u_value)
    extra32[2 * taps : 3 * taps] = high(w_u_value)
    extra32[27:28] = high(b_a_value)
    extra32[28:29] = b_a_value - high(b_a_value)
    extra32[29:30] = high(e_a_value)
    extra32[30:31] = e_a_value - high(e_a_value)
    extra32[31:32] = high(e_a_value)
    weight_a[taps * C :] = extra32[...].astype(BF16)
    for tap, copy in enumerate(copies):
        copy.wait()
        weight_back[tap * C : (tap + 1) * C, :] = weight_b[:, tap * C : (tap + 1) * C].T
    smalls[0].wait()


def train_kernel(
    dp_count,
    npatch,
    table_hbm,
    table,
    features,
    target32_hbm,
    weight_a_hbm,
    weight_b_hbm,
    weight_back_hbm,
    ends_hbm,
    grad_a,
    grad_b,
    send_out,
    loss_out,
    ints,
    chosen,
    blocks,
    target32,
    weight_a,
    weight_b,
    weight_back,
    ends,
    win_a,
    act,
    win_g,
    slope,
    aim,
    tails,
    int_sem,
    weight_sems,
    block_sems,
):
    devices = table.shape[0]
    slots = blocks.shape[0]
    taps = 9
    my_tile, my_dp = lax.axis_index("tile"), lax.axis_index("dp")
    my_core = lax.rem(my_tile * dp_count + my_dp, 2)

    copy_ints = pltpu.make_async_copy(table_hbm.at[:, 0, pl.ds(npatch * CELLS, C)], ints, int_sem)
    copy_ints.start()
    operands = (
        (target32_hbm, target32),
        (ends_hbm, ends),
        (weight_a_hbm, weight_a),
        (weight_b_hbm, weight_b),
        (weight_back_hbm, weight_back),
    )
    copies = [pltpu.make_async_copy(src, dst, weight_sems.at[at]) for at, (src, dst) in enumerate(operands)]
    for copy in copies:
        copy.start()
    copy_ints.wait()

    tile_name = my_tile.astype(F32)

    def choose(device, carry):
        turn, place_at = carry
        for patch in range(npatch):
            owned = ints[device, patch * FIELDS] == tile_name
            mine = jnp.logical_and(owned, turn == my_dp)
            chosen[jnp.where(mine, place_at, slots)] = device * npatch + patch
            place_at = jnp.where(mine, place_at + 1, place_at)
            following = jnp.where(turn == dp_count - 1, 0, turn + 1)
            turn = jnp.where(owned, following, turn)
        return turn, place_at


    def fields(slot):
        patch = chosen[slot]
        device = lax.div(patch, npatch)
        inner = lax.rem(patch, npatch)
        return device, inner

    def block_copy(slot):
        device, inner = fields(slot)
        row = ints[device, inner * FIELDS + 1].astype(jnp.int32)
        column = ints[device, inner * FIELDS + 2].astype(jnp.int32)
        most = (features.shape[1] - SPAN) // 16
        start = jnp.minimum(lax.shift_right_logical(column, 4), most) * 16
        start = pl.multiple_of(start, 16)
        copy = pltpu.make_async_copy(
            features.at[pl.ds(row, P_SIZE), pl.ds(start, SPAN)],
            blocks.at[slot],
            block_sems.at[slot],
        )
        return copy, row, column, column - start

    def start_block(slot, carry):
        block_copy(slot)[0].start()
        return carry

    turn, count = jnp.int32(0), jnp.int32(0)
    stops = [0, devices // 4, devices // 2, devices]
    for begin, end in zip(stops, stops[1:]):
        known = count
        turn, count = lax.fori_loop(begin, end, choose, (turn, known))
        lax.fori_loop(known, count, start_block, 0)

    @pl.when(count == 0)
    def _():
        grad_a[...] = jnp.zeros_like(grad_a)
        grad_b[...] = jnp.zeros_like(grad_b)
        tails[...] = jnp.zeros_like(tails)

    loss_out[...] = jnp.zeros_like(loss_out)
    edge = jnp.zeros((P_SIZE, 3 * C), BF16)
    for part in range(GROUP):
        first, last = part * CELLS, (part + 1) * CELLS - P_SIZE
        win_a[first : first + P_SIZE, : 3 * C] = edge
        win_a[last : last + P_SIZE, 6 * C : 9 * C] = edge
        win_g[last : last + P_SIZE, : 3 * C] = edge
        win_g[first : first + P_SIZE, 6 * C : 9 * C] = edge

    for copy in copies:
        copy.wait()

    cell_col = lax.broadcasted_iota(jnp.int32, (CELLS, C), 0) & (P_SIZE - 1)
    lane = lax.broadcasted_iota(jnp.int32, (CELLS, C), 1)
    lane_tap = lax.rem(lane, taps)
    lane_row, lane_col = lax.div(lane_tap, 3), lax.rem(lane_tap, 3)
    pick_shape = (P_SIZE, P_SIZE, C)
    tile_line = lax.broadcasted_iota(jnp.int32, (P_SIZE * SPAN // 8, 8, C), 1)
    pick_row = lax.broadcasted_iota(jnp.int32, pick_shape, 0) & 7
    pick_col = lax.broadcasted_iota(jnp.int32, pick_shape, 1)
    pick_lane = lax.broadcasted_iota(jnp.int32, pick_shape, 2)
    noise_pick = pick_lane == pick_row * P_SIZE + pick_col
    field_shape = (P_SIZE, P_SIZE, target32.shape[1])
    field_col = lax.broadcasted_iota(jnp.int32, field_shape, 1)
    field_lane = lax.broadcasted_iota(jnp.int32, field_shape, 2)
    loss_row = lax.broadcasted_iota(jnp.int32, loss_out.shape, 0)
    loss_lane = lax.broadcasted_iota(jnp.int32, loss_out.shape, 1)
    log_step = (math.log(SIGMA_HIGH) - math.log(SIGMA_LOW)) / (LEVELS - 1)

    def prepare(part, slot):
        base = part * CELLS
        copy, row, _, offset = block_copy(slot)
        device, inner = fields(slot)
        column = ints[device, inner * FIELDS + 2].astype(jnp.int32)
        level = ints[device, inner * FIELDS + 3]

        tiles = blocks[slot].astype(F32).reshape(P_SIZE * SPAN // 8, 8, C)
        within = offset & 7
        turned = pltpu.roll(tiles, (8 - within) & 7, 1)
        after = jnp.concatenate([turned[1:], turned[:1]], axis=0)
        tiles = jnp.where(tile_line + within < 8, turned, after).reshape(P_SIZE, SPAN // 8, 8, C)
        whole_tiles = lax.shift_right_logical(offset, 3)
        block = jnp.where(
            whole_tiles == 0,
            tiles[:, 0:2],
            jnp.where(whole_tiles == 1, tiles[:, 1:3], tiles[:, 2:4]),
        ).reshape(CELLS, C)
        for shift, value in enumerate(
            (from_previous_column(block, cell_col), block, from_next_column(block, cell_col))
        ):
            value = value.astype(BF16)
            for shift_row in range(3):
                store_window(win_a, base, 3 * shift_row + shift, value)

        log_sigma = math.log(SIGMA_LOW) + jnp.full((1, 1), level) * log_step
        sigma = jnp.exp(log_sigma)
        variance = sigma * sigma + SIGMA_DATA * SIGMA_DATA
        scale_in = 1.0 / jnp.sqrt(variance)
        embed = jnp.log(sigma) / 4.0

        tile_rows = target32.shape[0]
        lines = pltpu.roll(target32[...], lax.rem(tile_rows - row, tile_rows), 0)[:P_SIZE]
        clean = jnp.sum(
            jnp.where(field_lane == column + field_col, lines[:, None, :], 0.0),
            axis=2,
            keepdims=True,
        )
        at = pl.multiple_of(inner * CELLS, C)
        first = table[device, :, pl.ds(at, C)]
        second = table[device, :, pl.ds(pl.multiple_of(at + C, C), C)]
        half = (P_SIZE // 2, P_SIZE, C)
        drawn = jnp.concatenate(
            [jnp.broadcast_to(first[None], half), jnp.broadcast_to(second[None], half)], axis=0
        )
        noise = jnp.sum(jnp.where(noise_pick, drawn, 0.0), axis=2, keepdims=True)
        clean = jnp.broadcast_to(clean, pick_shape).reshape(CELLS, C)
        noise = jnp.broadcast_to(noise, pick_shape).reshape(CELLS, C)
        scaled = scale_in * (clean + sigma * noise)
        aim[base : base + CELLS] = scale_in * (2.0 * sigma * clean - 0.5 * noise)

        rows = jnp.where(
            lane_row == 0,
            from_previous_row(scaled),
            jnp.where(lane_row == 2, from_next_row(scaled), scaled),
        )
        moved = jnp.where(
            lane_col == 0,
            from_previous_column(rows, cell_col),
            jnp.where(lane_col == 2, from_next_column(rows, cell_col), rows),
        )
        moved_high = high(moved)
        value = jnp.where(lane < 2 * taps, moved_high, moved - moved_high)
        embed_high = high(embed)
        rest = jnp.where(
            lane < 29, 1.0, jnp.where(lane < 31, embed_high, embed - embed_high)
        )
        value = jnp.where(lane < 3 * taps, value, jnp.where(lane < 32, rest, 0.0))
        win_a[base : base + CELLS, taps * C :] = value.astype(BF16)

    def work(step, carry):
        slots_at = [step * GROUP + part for part in range(GROUP)]
        real = [slot < count for slot in slots_at]
        used = [jnp.minimum(slot, count - 1) for slot in slots_at]
        for part in range(GROUP):
            @pl.when(real[part])
            def _(part=part):
                block_copy(used[part])[0].wait()

        rows = [slice(part * CELLS, (part + 1) * CELLS) for part in range(GROUP)]

        def first_layer(part):
            return jnp.dot(win_a[rows[part]], weight_a[...], preferred_element_type=F32)

        def activate(part, pre_a):
            gate = sigmoid(pre_a)
            act[rows[part]] = (pre_a * gate).astype(BF16)
            slope[rows[part]] = gate * (1.0 + pre_a * (1.0 - gate))

        def second_layer(part):
            return jnp.dot(act[rows[part]], weight_b[...], preferred_element_type=F32)

        def finish(part, product):
            columns = []
            for shift in range(3):
                tap = [product[:, (3 * r + shift) * C : (3 * r + shift + 1) * C] for r in range(3)]
                columns.append(from_previous_row(tap[0]) + tap[1] + from_next_row(tap[2]))
            pre_b = (
                ends[0:1]
                + from_previous_column(columns[0], cell_col)
                + columns[1]
                + from_next_column(columns[2], cell_col)
            )
            gate = sigmoid(pre_b)
            final = jnp.sum(pre_b * gate * ends[1:2], axis=1, keepdims=True)
            residual = final - aim[rows[part]]
            device, inner = fields(used[part])
            weight = jnp.where(real[part], ints[device, inner * FIELDS + 4], 0.0)
            loss = weight * jnp.sum(residual * residual) * (1.0 / (CELLS * C))
            spot = jnp.logical_and(loss_row == device, loss_lane == inner)
            loss_out[...] += jnp.where(spot, loss, 0.0)
            factor = (2.0 / CELLS) * weight * residual
            grad_pre_b = factor * ends[1:2] * (gate * (1.0 + pre_b * (1.0 - gate)))
            base = part * CELLS
            for shift, value in enumerate(
                (
                    from_next_column(grad_pre_b, cell_col),
                    grad_pre_b,
                    from_previous_column(grad_pre_b, cell_col),
                )
            ):
                value = value.astype(BF16)
                for shift_row in range(3):
                    lanes = pl.ds((3 * shift_row + shift) * C, C)
                    if shift_row == 0:
                        win_g[base : base + CELLS - P_SIZE, lanes] = value[P_SIZE:]
                    elif shift_row == 1:
                        win_g[base : base + CELLS, lanes] = value
                    else:
                        win_g[base + P_SIZE : base + CELLS, lanes] = value[: CELLS - P_SIZE]

        def hidden(part):
            return jnp.dot(win_g[rows[part]], weight_back[...], preferred_element_type=F32)

        def turn_back(part, grad_hidden):
            return (grad_hidden * slope[rows[part]]).astype(BF16)

        prepare(0, used[0])
        pre_0 = first_layer(0)
        prepare(1, used[1])
        pre_1 = first_layer(1)
        activate(0, pre_0)
        product_0 = second_layer(0)
        activate(1, pre_1)
        product_1 = second_layer(1)
        finish(0, product_0)
        hidden_0 = hidden(0)
        finish(1, product_1)
        hidden_1 = hidden(1)
        back_0 = turn_back(0, hidden_0)
        started = step > 0
        over_cells = (((0,), (0,)), ((), ()))

        def add(at, grad, rows_of, columns_of):
            wide = columns_of[:, : 8 * C]
            grad[:, : 8 * C] = jnp.where(started, grad[:, : 8 * C], 0.0) + lax.dot_general(
                rows_of, wide, over_cells, preferred_element_type=F32
            )
            last = columns_of[:, 8 * C : 9 * C]
            tails[at] = jnp.where(started, tails[at], 0.0) + lax.dot_general(
                last, rows_of, over_cells, preferred_element_type=F32
            )

        add(1, grad_b, act[...], win_g)
        add(0, grad_a, jnp.concatenate([back_0, turn_back(1, hidden_1)], axis=0), win_a)
        return carry

    lax.fori_loop(0, lax.div(count + GROUP - 1, GROUP), work, 0)
    grad_a[:, 8 * C :] = tails[0].T
    grad_b[:, 8 * C :] = tails[1].T

    chunk = HID // devices
    for pair in range(devices // 2):
        for at, grad in ((0, grad_a), (taps * C, grad_b)):
            even = grad[2 * pair * chunk : (2 * pair + 1) * chunk]
            odd = grad[(2 * pair + 1) * chunk : (2 * pair + 2) * chunk]
            send_out[pair, :, pl.ds(at, taps * C)] = jnp.where(my_core == 0, odd, even).astype(BF16)


def halve_kernel(fan, kept, count, step, *refs):
    keeps, received, outs = refs[:kept], refs[kept : kept + count], refs[kept + count :]
    index = lax.axis_index("tile") * lax.axis_size("dp") + lax.axis_index("dp")
    mine = lax.rem(lax.div(index, step), fan)
    rows = outs[0].shape[0]
    width = outs[0].shape[2] // kept
    for peer in range(fan):
        low = jnp.bitwise_xor(mine, peer)
        for high_part in range(rows):
            at = high_part * fan + low
            for side, keep in enumerate(keeps):
                lanes = slice(side * width, (side + 1) * width)
                total = keep[2 * at + lax.rem(index, 2)] if kept > 1 else keep[at]
                for other in received:
                    total = total + other[at, :, lanes].astype(F32)
                outs[peer][high_part, :, lanes] = total.astype(outs[peer].dtype)


def finish_kernel(npatch, keep, losses, *refs):
    received, (grad, payload) = refs[:-2], refs[-2:]
    total = keep[0]
    for other in received:
        total = total + other[0].astype(F32)
    grad[...] = total
    half = total.shape[1] // 2
    lane = lax.broadcasted_iota(jnp.int32, losses.shape, 1)
    square_a = jnp.sum(total[:, :half] * total[:, :half])
    square_b = jnp.sum(total[:, half:] * total[:, half:])
    value = jnp.where(lane == npatch, square_a, losses[...])
    payload[:, 0, :] = jnp.where(lane == npatch + 1, square_b, value)


def scale_kernel(npatch, entries, grad, payload, losses, upd_a, upd_b):
    total = jnp.sum(payload[:, 0, :], axis=0, keepdims=True)
    lane = lax.broadcasted_iota(jnp.int32, total.shape, 1)
    for patch in range(npatch):
        losses[patch] = jnp.sum(jnp.where(lane == patch, total, 0.0))
    half = grad.shape[1] // 2
    for part, out in enumerate((upd_a, upd_b)):
        square = jnp.sum(jnp.where(lane == npatch + part, total, 0.0), axis=1, keepdims=True)
        out[...] = grad[:, part * half : (part + 1) * half] / jnp.sqrt(square / entries + EPSILON)


def local(
    features,
    target_field,
    owner_tile,
    row_offset,
    column_start,
    noise_level,
    icing_count,
    noise_draw,
    w_a,
    w_u,
    b_a,
    e_a,
    w_b,
    b_b,
    w_o,
):
    tile_count, dp_count = lax.axis_size("tile"), lax.axis_size("dp")
    devices = tile_count * dp_count
    npatch = owner_tile.shape[0]
    slots = max(2, 2 * npatch // tile_count) * devices // dp_count
    chunk = HID // devices
    width = 2 * 9 * C
    in_hbm = pl.BlockSpec(memory_space=pltpu.HBM)
    stay = functools.partial(pltpu.with_memory_space_constraint, memory_space=pltpu.HBM)
    in_vmem = pl.BlockSpec(memory_space=pltpu.VMEM)
    in_smem = pl.BlockSpec(memory_space=pltpu.SMEM)

    def room(mebibytes):
        return pltpu.CompilerParams(vmem_limit_bytes=mebibytes * 1024 * 1024)

    line = pl.pallas_call(
        pack_kernel,
        out_shape=jax.ShapeDtypeStruct((devices, 1, npatch * CELLS + C), F32),
        in_specs=[in_hbm] * 6,
        out_specs=in_vmem,
        scratch_shapes=[
            *[pltpu.SMEM((npatch,), jnp.int32)] * 5,
            pltpu.VMEM(noise_draw.shape, F32),
            pltpu.SemaphoreType.DMA((6,)),
        ],
        compiler_params=room(4),
        name="pack",
    )(
        *map(stay, (owner_tile.reshape(-1), row_offset, column_start, noise_level, icing_count, noise_draw))
    )
    table = lax.all_to_all(line, AXES, split_axis=0, concat_axis=0, tiled=True)

    weights = pl.pallas_call(
        weights_kernel,
        out_shape=(
            pltpu.HBM((10 * C, HID), BF16),
            pltpu.HBM((HID, 9 * C), BF16),
            pltpu.HBM((9 * C, HID), BF16),
            pltpu.HBM((2, C), F32),
            pltpu.HBM(target_field.shape, F32),
        ),
        in_specs=[in_hbm] * 8,
        out_specs=(in_vmem,) * 5,
        scratch_shapes=[
            pltpu.VMEM((9, HID), F32),
            pltpu.VMEM((1, HID), F32),
            pltpu.VMEM((1, HID), F32),
            pltpu.VMEM((C, HID), F32),
            pltpu.VMEM(target_field.shape, BF16),
            pltpu.SemaphoreType.DMA((16,)),
        ],
        compiler_params=room(8),
        name="weights",
    )(
        stay(w_a),
        stay(w_u),
        stay(b_a.reshape(1, -1)),
        stay(e_a.reshape(1, -1)),
        stay(w_b),
        stay(b_b.reshape(1, -1)),
        stay(w_o.reshape(1, -1)),
        stay(target_field),
    )
    weight_a, weight_b, weight_back, ends, target32 = weights

    grad_a, grad_b, send, losses = pl.pallas_call(
        functools.partial(train_kernel, dp_count, npatch),
        out_shape=(
            pltpu.VMEM((HID, 9 * C), F32),
            pltpu.VMEM((HID, 9 * C), F32),
            pltpu.VMEM((devices // 2, chunk, width), BF16),
            pltpu.VMEM((devices, C), F32),
        ),
        in_specs=[in_hbm, in_vmem] + [in_hbm] * 6,
        out_specs=(in_vmem,) * 4,
        scratch_shapes=[
            pltpu.SMEM((devices, C), F32),
            pltpu.SMEM((slots + 1,), jnp.int32),
            pltpu.VMEM((slots, P_SIZE, SPAN, C), BF16),
            pltpu.VMEM(target_field.shape, F32),
            pltpu.VMEM((10 * C, HID), BF16),
            pltpu.VMEM((HID, 9 * C), BF16),
            pltpu.VMEM((9 * C, HID), BF16),
            pltpu.VMEM((2, C), F32),
            pltpu.VMEM((GROUP * CELLS, 10 * C), BF16),
            pltpu.VMEM((GROUP * CELLS, HID), BF16),
            pltpu.VMEM((GROUP * CELLS, 9 * C), BF16),
            pltpu.VMEM((GROUP * CELLS, HID), F32),
            pltpu.VMEM((GROUP * CELLS, C), F32),
            pltpu.VMEM((2, C, HID), F32),
            pltpu.SemaphoreType.DMA,
            pltpu.SemaphoreType.DMA((5,)),
            pltpu.SemaphoreType.DMA((slots,)),
        ],
        compiler_params=room(32),
        name="train",
    )(table, table, *map(stay, (features, target32, weight_a, weight_b, weight_back, ends)))

    def exchange(array, distance):
        return lax.ppermute(array, AXES, [(i, i ^ distance) for i in range(devices)])

    received = [exchange(send, 1)]
    keeps = [grad.reshape(devices, chunk, 9 * C) for grad in (grad_a, grad_b)]
    rows = devices // 2
    step = 2
    while step < devices:
        fan = min(8, devices // step)
        rows //= fan
        part = (rows, chunk, width)
        outs = pl.pallas_call(
            functools.partial(halve_kernel, fan, len(keeps), len(received), step),
            out_shape=(
                pltpu.VMEM(part, F32),
                *[pltpu.VMEM(part, BF16) for _ in range(fan - 1)],
            ),
            in_specs=[in_vmem] * (len(keeps) + len(received)),
            out_specs=(in_vmem,) * fan,
            compiler_params=room(16),
            name=f"halve_{step}",
        )(*keeps, *received)
        keeps = outs[:1]
        order = sorted(range(1, fan), key=lambda peer: ((0, 0, 2, 1)[peer.bit_count()], peer))
        received = [exchange(outs[peer], peer * step) for peer in order]
        step *= fan

    grad, payload = pl.pallas_call(
        functools.partial(finish_kernel, npatch),
        out_shape=(
            pltpu.VMEM((chunk, width), F32),
            pltpu.VMEM((devices, 1, C), F32),
        ),
        in_specs=[in_vmem] * (2 + len(received)),
        out_specs=(in_vmem, in_vmem),
        compiler_params=room(4),
        name="finish",
    )(*keeps, losses, *received)
    payload = lax.all_to_all(payload, AXES, split_axis=0, concat_axis=0, tiled=True)
    out = jax.ShapeDtypeStruct((chunk, width // 2), F32)
    sums, upd_a, upd_b = pl.pallas_call(
        functools.partial(scale_kernel, npatch, HID * 9 * C),
        out_shape=(jax.ShapeDtypeStruct((npatch,), F32), out, out),
        in_specs=[in_vmem, in_vmem],
        out_specs=(in_smem, in_vmem, in_vmem),
        compiler_params=room(4),
        name="scale",
    )(grad, payload)
    return sums, upd_a, upd_b


def solution(mesh):
    both = P(AXES)
    return jax.shard_map(
        local,
        mesh=mesh,
        in_specs=(
            P("tile", None, None),
            P("tile", None),
            P(AXES, None),
            both,
            both,
            both,
            both,
            P(AXES, None, None),
            P(),
            P(),
            P(),
            P(),
            P(),
            P(),
            P(),
        ),
        out_specs=(both, P(AXES, None), P(AXES, None)),
        check_vma=False,
    )
```

```python
import functools
import math

import jax
import jax.numpy as jnp
from jax import lax
from jax.experimental import pallas as pl
from jax.experimental.pallas import tpu as pltpu
from jax.sharding import PartitionSpec as P

C = 128
HID = 512
P_SIZE = 16
LEVELS = 32
CELLS = P_SIZE * P_SIZE
SPAN = 32
FIELDS = 8
GROUP = 2

SIGMA_LOW = 0.02
SIGMA_HIGH = 80.0
SIGMA_DATA = 0.5
EPSILON = 1e-06
AXES = ("tile", "dp")
BF16 = jnp.bfloat16
F32 = jnp.float32


def sigmoid(values):
    return 0.5 * jnp.tanh(0.5 * values) + 0.5


def from_previous_column(x, col):
    return jnp.where(col == 0, 0.0, pltpu.roll(x, 1, 0))


def from_next_column(x, col):
    return jnp.where(col == P_SIZE - 1, 0.0, pltpu.roll(x, x.shape[0] - 1, 0))


def from_previous_row(x):
    zero = jnp.zeros((P_SIZE, x.shape[1]), x.dtype)
    parts = []
    for at in range(0, x.shape[0], CELLS):
        parts += [zero, x[at : at + CELLS - P_SIZE]]
    return jnp.concatenate(parts, axis=0)


def from_next_row(x):
    zero = jnp.zeros((P_SIZE, x.shape[1]), x.dtype)
    parts = []
    for at in range(0, x.shape[0], CELLS):
        parts += [x[at + P_SIZE : at + CELLS], zero]
    return jnp.concatenate(parts, axis=0)


def high(value):
    return value.astype(BF16).astype(F32)


def store_window(ref, base, tap, rows):
    lanes = pl.ds(tap * C, C)
    shift = tap // 3
    if shift == 0:
        ref[base + P_SIZE : base + CELLS, lanes] = rows[: CELLS - P_SIZE]
    elif shift == 1:
        ref[base : base + CELLS, lanes] = rows
    else:
        ref[base : base + CELLS - P_SIZE, lanes] = rows[P_SIZE:]


def pack_kernel(*refs):
    sources, line, scratch, sems = refs[:6], refs[6], refs[7:13], refs[13]
    copies = [
        pltpu.make_async_copy(src, dst, sems.at[at]) for at, (src, dst) in enumerate(zip(sources, scratch))
    ]
    for copy in copies:
        copy.start()
    *integers, drawn = scratch
    npatch = drawn.shape[0]
    lane = lax.broadcasted_iota(jnp.int32, (1, C), 1)
    numbers = jnp.zeros((1, C), jnp.int32)
    for copy in copies:
        copy.wait()
    for patch in range(npatch):
        for at, ref in enumerate(integers):
            numbers = jnp.where(lane == patch * FIELDS + at, ref[patch], numbers)
    shape = (line.shape[0], 1, C)
    line[:, :, npatch * CELLS :] = jnp.broadcast_to(numbers.astype(F32)[None], shape)
    rows = C // P_SIZE
    mine = lax.broadcasted_iota(jnp.int32, (rows, C), 0)
    here = lax.broadcasted_iota(jnp.int32, (rows, C), 1) // P_SIZE == mine
    for patch in range(npatch):
        for at in range(0, P_SIZE, rows):
            part = drawn[patch, at : at + rows, :]
            spread = jnp.concatenate([part] * rows, axis=1)
            flat = jnp.sum(jnp.where(here, spread, 0.0), axis=0, keepdims=True)
            start = patch * CELLS + at * P_SIZE
            line[:, :, start : start + C] = jnp.broadcast_to(flat[None], shape)


def weights_kernel(
    w_a, w_u, b_a, e_a, w_b, b_b, w_o, target,
    weight_a, weight_b, weight_back, ends, target32,
    small_u, small_b, small_e, extra32, field, sems,
):
    taps = 9
    copies = [
        pltpu.make_async_copy(w_b.at[pl.ds(tap * HID, HID)], weight_b.at[:, pl.ds(tap * C, C)], sems.at[tap])
        for tap in range(taps)
    ]
    places = (
        (w_a, weight_a.at[pl.ds(0, taps * C)]),
        (w_u, small_u),
        (b_a, small_b),
        (e_a, small_e),
        (b_b, ends.at[pl.ds(0, 1)]),
        (w_o, ends.at[pl.ds(1, 1)]),
        (target, field),
    )
    smalls = [pltpu.make_async_copy(src, dst, sems.at[taps + at]) for at, (src, dst) in enumerate(places)]
    for copy in smalls + copies:
        copy.start()
    for copy in smalls[1:]:
        copy.wait()
    target32[...] = field[...].astype(F32)
    extra32[...] = jnp.zeros_like(extra32)
    w_u_value, b_a_value, e_a_value = small_u[...], small_b[...], small_e[...]
    extra32[0:taps] = high(w_u_value)
    extra32[taps : 2 * taps] = w_u_value - high(w_u_value)
    extra32[2 * taps : 3 * taps] = high(w_u_value)
    extra32[27:28] = high(b_a_value)
    extra32[28:29] = b_a_value - high(b_a_value)
    extra32[29:30] = high(e_a_value)
    extra32[30:31] = e_a_value - high(e_a_value)
    extra32[31:32] = high(e_a_value)
    weight_a[taps * C :] = extra32[...].astype(BF16)
    for tap, copy in enumerate(copies):
        copy.wait()
        weight_back[tap * C : (tap + 1) * C, :] = weight_b[:, tap * C : (tap + 1) * C].T
    smalls[0].wait()


def train_kernel(
    dp_count,
    npatch,
    table_hbm,
    table,
    features,
    target32_hbm,
    weight_a_hbm,
    weight_b_hbm,
    weight_back_hbm,
    ends_hbm,
    grad_a,
    grad_b,
    send_out,
    loss_out,
    ints,
    chosen,
    blocks,
    target32,
    weight_a,
    weight_b,
    weight_back,
    ends,
    win_a,
    act,
    win_g,
    slope,
    aim,
    tails,
    int_sem,
    weight_sems,
    block_sems,
):
    devices = table.shape[0]
    slots = blocks.shape[0]
    taps = 9
    my_tile, my_dp = lax.axis_index("tile"), lax.axis_index("dp")
    my_core = lax.rem(my_tile * dp_count + my_dp, 2)

    copy_ints = pltpu.make_async_copy(table_hbm.at[:, 0, pl.ds(npatch * CELLS, C)], ints, int_sem)
    copy_ints.start()
    operands = (
        (target32_hbm, target32),
        (ends_hbm, ends),
        (weight_a_hbm, weight_a),
        (weight_b_hbm, weight_b),
        (weight_back_hbm, weight_back),
    )
    copies = [pltpu.make_async_copy(src, dst, weight_sems.at[at]) for at, (src, dst) in enumerate(operands)]
    for copy in copies:
        copy.start()
    copy_ints.wait()

    tile_name = my_tile.astype(F32)

    def choose(device, carry):
        turn, place_at = carry
        for patch in range(npatch):
            owned = ints[device, patch * FIELDS] == tile_name
            mine = jnp.logical_and(owned, turn == my_dp)
            chosen[jnp.where(mine, place_at, slots)] = device * npatch + patch
            place_at = jnp.where(mine, place_at + 1, place_at)
            following = jnp.where(turn == dp_count - 1, 0, turn + 1)
            turn = jnp.where(owned, following, turn)
        return turn, place_at


    def fields(slot):
        patch = chosen[slot]
        device = lax.div(patch, npatch)
        inner = lax.rem(patch, npatch)
        return device, inner

    def block_copy(slot):
        device, inner = fields(slot)
        row = ints[device, inner * FIELDS + 1].astype(jnp.int32)
        column = ints[device, inner * FIELDS + 2].astype(jnp.int32)
        most = (features.shape[1] - SPAN) // 16
        start = jnp.minimum(lax.shift_right_logical(column, 4), most) * 16
        start = pl.multiple_of(start, 16)
        copy = pltpu.make_async_copy(
            features.at[pl.ds(row, P_SIZE), pl.ds(start, SPAN)],
            blocks.at[slot],
            block_sems.at[slot],
        )
        return copy, row, column, column - start

    def start_block(slot, carry):
        block_copy(slot)[0].start()
        return carry

    turn, count = jnp.int32(0), jnp.int32(0)
    stops = [0, devices // 4, devices // 2, devices]
    for begin, end in zip(stops, stops[1:]):
        known = count
        turn, count = lax.fori_loop(begin, end, choose, (turn, known))
        lax.fori_loop(known, count, start_block, 0)

    @pl.when(count == 0)
    def _():
        grad_a[...] = jnp.zeros_like(grad_a)
        grad_b[...] = jnp.zeros_like(grad_b)
        tails[...] = jnp.zeros_like(tails)

    loss_out[...] = jnp.zeros_like(loss_out)
    edge = jnp.zeros((P_SIZE, 3 * C), BF16)
    for part in range(GROUP):
        first, last = part * CELLS, (part + 1) * CELLS - P_SIZE
        win_a[first : first + P_SIZE, : 3 * C] = edge
        win_a[last : last + P_SIZE, 6 * C : 9 * C] = edge
        win_g[last : last + P_SIZE, : 3 * C] = edge
        win_g[first : first + P_SIZE, 6 * C : 9 * C] = edge

    for copy in copies:
        copy.wait()

    cell_col = lax.broadcasted_iota(jnp.int32, (CELLS, C), 0) & (P_SIZE - 1)
    lane = lax.broadcasted_iota(jnp.int32, (CELLS, C), 1)
    lane_tap = lax.rem(lane, taps)
    lane_row, lane_col = lax.div(lane_tap, 3), lax.rem(lane_tap, 3)
    pick_shape = (P_SIZE, P_SIZE, C)
    tile_line = lax.broadcasted_iota(jnp.int32, (P_SIZE * SPAN // 8, 8, C), 1)
    pick_row = lax.broadcasted_iota(jnp.int32, pick_shape, 0) & 7
    pick_col = lax.broadcasted_iota(jnp.int32, pick_shape, 1)
    pick_lane = lax.broadcasted_iota(jnp.int32, pick_shape, 2)
    noise_pick = pick_lane == pick_row * P_SIZE + pick_col
    field_shape = (P_SIZE, P_SIZE, target32.shape[1])
    field_col = lax.broadcasted_iota(jnp.int32, field_shape, 1)
    field_lane = lax.broadcasted_iota(jnp.int32, field_shape, 2)
    loss_row = lax.broadcasted_iota(jnp.int32, loss_out.shape, 0)
    loss_lane = lax.broadcasted_iota(jnp.int32, loss_out.shape, 1)
    log_step = (math.log(SIGMA_HIGH) - math.log(SIGMA_LOW)) / (LEVELS - 1)

    def prepare(part, slot):
        base = part * CELLS
        copy, row, _, offset = block_copy(slot)
        device, inner = fields(slot)
        column = ints[device, inner * FIELDS + 2].astype(jnp.int32)
        level = ints[device, inner * FIELDS + 3]

        tiles = blocks[slot].astype(F32).reshape(P_SIZE * SPAN // 8, 8, C)
        within = offset & 7
        turned = pltpu.roll(tiles, (8 - within) & 7, 1)
        after = jnp.concatenate([turned[1:], turned[:1]], axis=0)
        tiles = jnp.where(tile_line + within < 8, turned, after).reshape(P_SIZE, SPAN // 8, 8, C)
        whole_tiles = lax.shift_right_logical(offset, 3)
        block = jnp.where(
            whole_tiles == 0,
            tiles[:, 0:2],
            jnp.where(whole_tiles == 1, tiles[:, 1:3], tiles[:, 2:4]),
        ).reshape(CELLS, C)
        for shift, value in enumerate(
            (from_previous_column(block, cell_col), block, from_next_column(block, cell_col))
        ):
            value = value.astype(BF16)
            for shift_row in range(3):
                store_window(win_a, base, 3 * shift_row + shift, value)

        log_sigma = math.log(SIGMA_LOW) + jnp.full((1, 1), level) * log_step
        sigma = jnp.exp(log_sigma)
        variance = sigma * sigma + SIGMA_DATA * SIGMA_DATA
        scale_in = 1.0 / jnp.sqrt(variance)
        embed = jnp.log(sigma) / 4.0

        tile_rows = target32.shape[0]
        lines = pltpu.roll(target32[...], lax.rem(tile_rows - row, tile_rows), 0)[:P_SIZE]
        clean = jnp.sum(
            jnp.where(field_lane == column + field_col, lines[:, None, :], 0.0),
            axis=2,
            keepdims=True,
        )
        at = pl.multiple_of(inner * CELLS, C)
        first = table[device, :, pl.ds(at, C)]
        second = table[device, :, pl.ds(pl.multiple_of(at + C, C), C)]
        half = (P_SIZE // 2, P_SIZE, C)
        drawn = jnp.concatenate(
            [jnp.broadcast_to(first[None], half), jnp.broadcast_to(second[None], half)], axis=0
        )
        noise = jnp.sum(jnp.where(noise_pick, drawn, 0.0), axis=2, keepdims=True)
        clean = jnp.broadcast_to(clean, pick_shape).reshape(CELLS, C)
        noise = jnp.broadcast_to(noise, pick_shape).reshape(CELLS, C)
        scaled = scale_in * (clean + sigma * noise)
        aim[base : base + CELLS] = scale_in * (2.0 * sigma * clean - 0.5 * noise)

        rows = jnp.where(
            lane_row == 0,
            from_previous_row(scaled),
            jnp.where(lane_row == 2, from_next_row(scaled), scaled),
        )
        moved = jnp.where(
            lane_col == 0,
            from_previous_column(rows, cell_col),
            jnp.where(lane_col == 2, from_next_column(rows, cell_col), rows),
        )
        moved_high = high(moved)
        value = jnp.where(lane < 2 * taps, moved_high, moved - moved_high)
        embed_high = high(embed)
        rest = jnp.where(
            lane < 29, 1.0, jnp.where(lane < 31, embed_high, embed - embed_high)
        )
        value = jnp.where(lane < 3 * taps, value, jnp.where(lane < 32, rest, 0.0))
        win_a[base : base + CELLS, taps * C :] = value.astype(BF16)

    def work(step, carry):
        slots_at = [step * GROUP + part for part in range(GROUP)]
        real = [slot < count for slot in slots_at]
        used = [jnp.minimum(slot, count - 1) for slot in slots_at]
        for part in range(GROUP):
            @pl.when(real[part])
            def _(part=part):
                block_copy(used[part])[0].wait()

        rows = [slice(part * CELLS, (part + 1) * CELLS) for part in range(GROUP)]

        def first_layer(part):
            return jnp.dot(win_a[rows[part]], weight_a[...], preferred_element_type=F32)

        def activate(part, pre_a):
            gate = sigmoid(pre_a)
            act[rows[part]] = (pre_a * gate).astype(BF16)
            slope[rows[part]] = gate * (1.0 + pre_a * (1.0 - gate))

        def second_layer(part):
            mine = act[rows[part]]
            wide = jnp.dot(mine, weight_b[:, : 8 * C], preferred_element_type=F32)
            last = lax.dot_general(
                weight_back[8 * C :], mine, (((1,), (1,)), ((), ())), preferred_element_type=F32
            )
            return [wide[:, tap * C : (tap + 1) * C] for tap in range(8)] + [last.T]

        def finish(part, product):
            columns = []
            for shift in range(3):
                tap = [product[3 * r + shift] for r in range(3)]
                columns.append(from_previous_row(tap[0]) + tap[1] + from_next_row(tap[2]))
            pre_b = (
                ends[0:1]
                + from_previous_column(columns[0], cell_col)
                + columns[1]
                + from_next_column(columns[2], cell_col)
            )
            gate = sigmoid(pre_b)
            final = jnp.sum(pre_b * gate * ends[1:2], axis=1, keepdims=True)
            residual = final - aim[rows[part]]
            device, inner = fields(used[part])
            weight = jnp.where(real[part], ints[device, inner * FIELDS + 4], 0.0)
            loss = weight * jnp.sum(residual * residual) * (1.0 / (CELLS * C))
            spot = jnp.logical_and(loss_row == device, loss_lane == inner)
            loss_out[...] += jnp.where(spot, loss, 0.0)
            factor = (2.0 / CELLS) * weight * residual
            grad_pre_b = factor * ends[1:2] * (gate * (1.0 + pre_b * (1.0 - gate)))
            base = part * CELLS
            for shift, value in enumerate(
                (
                    from_next_column(grad_pre_b, cell_col),
                    grad_pre_b,
                    from_previous_column(grad_pre_b, cell_col),
                )
            ):
                value = value.astype(BF16)
                for shift_row in range(3):
                    lanes = pl.ds((3 * shift_row + shift) * C, C)
                    if shift_row == 0:
                        win_g[base : base + CELLS - P_SIZE, lanes] = value[P_SIZE:]
                    elif shift_row == 1:
                        win_g[base : base + CELLS, lanes] = value
                    else:
                        win_g[base + P_SIZE : base + CELLS, lanes] = value[: CELLS - P_SIZE]

        def hidden(part):
            return jnp.dot(win_g[rows[part]], weight_back[...], preferred_element_type=F32)

        def turn_back(part, grad_hidden):
            return (grad_hidden * slope[rows[part]]).astype(BF16)

        prepare(0, used[0])
        pre_0 = first_layer(0)
        prepare(1, used[1])
        pre_1 = first_layer(1)
        activate(0, pre_0)
        product_0 = second_layer(0)
        activate(1, pre_1)
        product_1 = second_layer(1)
        finish(0, product_0)
        hidden_0 = hidden(0)
        finish(1, product_1)
        hidden_1 = hidden(1)
        back_0 = turn_back(0, hidden_0)
        started = step > 0
        over_cells = (((0,), (0,)), ((), ()))

        def add(at, grad, rows_of, columns_of):
            wide = columns_of[:, : 8 * C]
            grad[:, : 8 * C] = jnp.where(started, grad[:, : 8 * C], 0.0) + lax.dot_general(
                rows_of, wide, over_cells, preferred_element_type=F32
            )
            last = columns_of[:, 8 * C : 9 * C]
            tails[at] = jnp.where(started, tails[at], 0.0) + lax.dot_general(
                last, rows_of, over_cells, preferred_element_type=F32
            )

        add(1, grad_b, act[...], win_g)
        add(0, grad_a, jnp.concatenate([back_0, turn_back(1, hidden_1)], axis=0), win_a)
        return carry

    lax.fori_loop(0, lax.div(count + GROUP - 1, GROUP), work, 0)
    grad_a[:, 8 * C :] = tails[0].T
    grad_b[:, 8 * C :] = tails[1].T

    chunk = HID // devices
    for pair in range(devices // 2):
        for at, grad in ((0, grad_a), (taps * C, grad_b)):
            even = grad[2 * pair * chunk : (2 * pair + 1) * chunk]
            odd = grad[(2 * pair + 1) * chunk : (2 * pair + 2) * chunk]
            send_out[pair, :, pl.ds(at, taps * C)] = jnp.where(my_core == 0, odd, even).astype(BF16)


def halve_kernel(fan, kept, count, step, *refs):
    keeps, received, outs = refs[:kept], refs[kept : kept + count], refs[kept + count :]
    index = lax.axis_index("tile") * lax.axis_size("dp") + lax.axis_index("dp")
    mine = lax.rem(lax.div(index, step), fan)
    rows = outs[0].shape[0]
    width = outs[0].shape[2] // kept
    for peer in range(fan):
        low = jnp.bitwise_xor(mine, peer)
        for high_part in range(rows):
            at = high_part * fan + low
            for side, keep in enumerate(keeps):
                lanes = slice(side * width, (side + 1) * width)
                total = keep[2 * at + lax.rem(index, 2)] if kept > 1 else keep[at]
                for other in received:
                    total = total + other[at, :, lanes].astype(F32)
                outs[peer][high_part, :, lanes] = total.astype(outs[peer].dtype)


def finish_kernel(npatch, keep, losses, *refs):
    received, (grad, payload) = refs[:-2], refs[-2:]
    total = keep[0]
    for other in received:
        total = total + other[0].astype(F32)
    grad[...] = total
    half = total.shape[1] // 2
    lane = lax.broadcasted_iota(jnp.int32, losses.shape, 1)
    square_a = jnp.sum(total[:, :half] * total[:, :half])
    square_b = jnp.sum(total[:, half:] * total[:, half:])
    value = jnp.where(lane == npatch, square_a, losses[...])
    payload[:, 0, :] = jnp.where(lane == npatch + 1, square_b, value)


def scale_kernel(npatch, entries, grad, payload, losses, upd_a, upd_b):
    total = jnp.sum(payload[:, 0, :], axis=0, keepdims=True)
    lane = lax.broadcasted_iota(jnp.int32, total.shape, 1)
    for patch in range(npatch):
        losses[patch] = jnp.sum(jnp.where(lane == patch, total, 0.0))
    half = grad.shape[1] // 2
    for part, out in enumerate((upd_a, upd_b)):
        square = jnp.sum(jnp.where(lane == npatch + part, total, 0.0), axis=1, keepdims=True)
        out[...] = grad[:, part * half : (part + 1) * half] / jnp.sqrt(square / entries + EPSILON)


def local(
    features,
    target_field,
    owner_tile,
    row_offset,
    column_start,
    noise_level,
    icing_count,
    noise_draw,
    w_a,
    w_u,
    b_a,
    e_a,
    w_b,
    b_b,
    w_o,
):
    tile_count, dp_count = lax.axis_size("tile"), lax.axis_size("dp")
    devices = tile_count * dp_count
    npatch = owner_tile.shape[0]
    slots = max(2, 2 * npatch // tile_count) * devices // dp_count
    chunk = HID // devices
    width = 2 * 9 * C
    in_hbm = pl.BlockSpec(memory_space=pltpu.HBM)
    stay = functools.partial(pltpu.with_memory_space_constraint, memory_space=pltpu.HBM)
    in_vmem = pl.BlockSpec(memory_space=pltpu.VMEM)
    in_smem = pl.BlockSpec(memory_space=pltpu.SMEM)

    def room(mebibytes):
        return pltpu.CompilerParams(vmem_limit_bytes=mebibytes * 1024 * 1024)

    line = pl.pallas_call(
        pack_kernel,
        out_shape=jax.ShapeDtypeStruct((devices, 1, npatch * CELLS + C), F32),
        in_specs=[in_hbm] * 6,
        out_specs=in_vmem,
        scratch_shapes=[
            *[pltpu.SMEM((npatch,), jnp.int32)] * 5,
            pltpu.VMEM(noise_draw.shape, F32),
            pltpu.SemaphoreType.DMA((6,)),
        ],
        compiler_params=room(4),
        name="pack",
    )(
        *map(stay, (owner_tile.reshape(-1), row_offset, column_start, noise_level, icing_count, noise_draw))
    )
    table = lax.all_to_all(line, AXES, split_axis=0, concat_axis=0, tiled=True)

    weights = pl.pallas_call(
        weights_kernel,
        out_shape=(
            pltpu.HBM((10 * C, HID), BF16),
            pltpu.HBM((HID, 9 * C), BF16),
            pltpu.HBM((9 * C, HID), BF16),
            pltpu.HBM((2, C), F32),
            pltpu.HBM(target_field.shape, F32),
        ),
        in_specs=[in_hbm] * 8,
        out_specs=(in_vmem,) * 5,
        scratch_shapes=[
            pltpu.VMEM((9, HID), F32),
            pltpu.VMEM((1, HID), F32),
            pltpu.VMEM((1, HID), F32),
            pltpu.VMEM((C, HID), F32),
            pltpu.VMEM(target_field.shape, BF16),
            pltpu.SemaphoreType.DMA((16,)),
        ],
        compiler_params=room(8),
        name="weights",
    )(
        stay(w_a),
        stay(w_u),
        stay(b_a.reshape(1, -1)),
        stay(e_a.reshape(1, -1)),
        stay(w_b),
        stay(b_b.reshape(1, -1)),
        stay(w_o.reshape(1, -1)),
        stay(target_field),
    )
    weight_a, weight_b, weight_back, ends, target32 = weights

    grad_a, grad_b, send, losses = pl.pallas_call(
        functools.partial(train_kernel, dp_count, npatch),
        out_shape=(
            pltpu.VMEM((HID, 9 * C), F32),
            pltpu.VMEM((HID, 9 * C), F32),
            pltpu.VMEM((devices // 2, chunk, width), BF16),
            pltpu.VMEM((devices, C), F32),
        ),
        in_specs=[in_hbm, in_vmem] + [in_hbm] * 6,
        out_specs=(in_vmem,) * 4,
        scratch_shapes=[
            pltpu.SMEM((devices, C), F32),
            pltpu.SMEM((slots + 1,), jnp.int32),
            pltpu.VMEM((slots, P_SIZE, SPAN, C), BF16),
            pltpu.VMEM(target_field.shape, F32),
            pltpu.VMEM((10 * C, HID), BF16),
            pltpu.VMEM((HID, 9 * C), BF16),
            pltpu.VMEM((9 * C, HID), BF16),
            pltpu.VMEM((2, C), F32),
            pltpu.VMEM((GROUP * CELLS, 10 * C), BF16),
            pltpu.VMEM((GROUP * CELLS, HID), BF16),
            pltpu.VMEM((GROUP * CELLS, 9 * C), BF16),
            pltpu.VMEM((GROUP * CELLS, HID), F32),
            pltpu.VMEM((GROUP * CELLS, C), F32),
            pltpu.VMEM((2, C, HID), F32),
            pltpu.SemaphoreType.DMA,
            pltpu.SemaphoreType.DMA((5,)),
            pltpu.SemaphoreType.DMA((slots,)),
        ],
        compiler_params=room(32),
        name="train",
    )(table, table, *map(stay, (features, target32, weight_a, weight_b, weight_back, ends)))

    def exchange(array, distance):
        return lax.ppermute(array, AXES, [(i, i ^ distance) for i in range(devices)])

    received = [exchange(send, 1)]
    keeps = [grad.reshape(devices, chunk, 9 * C) for grad in (grad_a, grad_b)]
    rows = devices // 2
    step = 2
    while step < devices:
        fan = min(8, devices // step)
        rows //= fan
        part = (rows, chunk, width)
        outs = pl.pallas_call(
            functools.partial(halve_kernel, fan, len(keeps), len(received), step),
            out_shape=(
                pltpu.VMEM(part, F32),
                *[pltpu.VMEM(part, BF16) for _ in range(fan - 1)],
            ),
            in_specs=[in_vmem] * (len(keeps) + len(received)),
            out_specs=(in_vmem,) * fan,
            compiler_params=room(16),
            name=f"halve_{step}",
        )(*keeps, *received)
        keeps = outs[:1]
        order = sorted(range(1, fan), key=lambda peer: ((0, 0, 2, 1)[peer.bit_count()], peer))
        received = [exchange(outs[peer], peer * step) for peer in order]
        step *= fan

    grad, payload = pl.pallas_call(
        functools.partial(finish_kernel, npatch),
        out_shape=(
            pltpu.VMEM((chunk, width), F32),
            pltpu.VMEM((devices, 1, C), F32),
        ),
        in_specs=[in_vmem] * (2 + len(received)),
        out_specs=(in_vmem, in_vmem),
        compiler_params=room(4),
        name="finish",
    )(*keeps, losses, *received)
    payload = lax.all_to_all(payload, AXES, split_axis=0, concat_axis=0, tiled=True)
    out = jax.ShapeDtypeStruct((chunk, width // 2), F32)
    sums, upd_a, upd_b = pl.pallas_call(
        functools.partial(scale_kernel, npatch, HID * 9 * C),
        out_shape=(jax.ShapeDtypeStruct((npatch,), F32), out, out),
        in_specs=[in_vmem, in_vmem],
        out_specs=(in_smem, in_vmem, in_vmem),
        compiler_params=room(4),
        name="scale",
    )(grad, payload)
    return sums, upd_a, upd_b


def solution(mesh):
    both = P(AXES)
    return jax.shard_map(
        local,
        mesh=mesh,
        in_specs=(
            P("tile", None, None),
            P("tile", None),
            P(AXES, None),
            both,
            both,
            both,
            both,
            P(AXES, None, None),
            P(),
            P(),
            P(),
            P(),
            P(),
            P(),
            P(),
        ),
        out_specs=(both, P(AXES, None), P(AXES, None)),
        check_vma=False,
    )
```

```python
import functools
import math

import jax
import jax.numpy as jnp
from jax import lax
from jax.experimental import pallas as pl
from jax.experimental.pallas import tpu as pltpu
from jax.sharding import PartitionSpec as P

C = 128
HID = 512
P_SIZE = 16
LEVELS = 32
CELLS = P_SIZE * P_SIZE
SPAN = 32
FIELDS = 8
GROUP = 2

SIGMA_LOW = 0.02
SIGMA_HIGH = 80.0
SIGMA_DATA = 0.5
EPSILON = 1e-06
AXES = ("tile", "dp")
BF16 = jnp.bfloat16
F32 = jnp.float32


def sigmoid(values):
    return 0.5 * jnp.tanh(0.5 * values) + 0.5


def from_previous_column(x, col):
    return jnp.where(col == 0, 0.0, pltpu.roll(x, 1, 0))


def from_next_column(x, col):
    return jnp.where(col == P_SIZE - 1, 0.0, pltpu.roll(x, x.shape[0] - 1, 0))


def from_previous_row(x):
    zero = jnp.zeros((P_SIZE, x.shape[1]), x.dtype)
    parts = []
    for at in range(0, x.shape[0], CELLS):
        parts += [zero, x[at : at + CELLS - P_SIZE]]
    return jnp.concatenate(parts, axis=0)


def from_next_row(x):
    zero = jnp.zeros((P_SIZE, x.shape[1]), x.dtype)
    parts = []
    for at in range(0, x.shape[0], CELLS):
        parts += [x[at + P_SIZE : at + CELLS], zero]
    return jnp.concatenate(parts, axis=0)


def high(value):
    return value.astype(BF16).astype(F32)


def store_window(ref, base, tap, rows):
    lanes = pl.ds(tap * C, C)
    shift = tap // 3
    if shift == 0:
        ref[base + P_SIZE : base + CELLS, lanes] = rows[: CELLS - P_SIZE]
    elif shift == 1:
        ref[base : base + CELLS, lanes] = rows
    else:
        ref[base : base + CELLS - P_SIZE, lanes] = rows[P_SIZE:]


def pack_kernel(*refs):
    sources, line, scratch, sems = refs[:6], refs[6], refs[7:13], refs[13]
    copies = [
        pltpu.make_async_copy(src, dst, sems.at[at]) for at, (src, dst) in enumerate(zip(sources, scratch))
    ]
    for copy in copies:
        copy.start()
    *integers, drawn = scratch
    npatch = drawn.shape[0]
    lane = lax.broadcasted_iota(jnp.int32, (1, C), 1)
    numbers = jnp.zeros((1, C), jnp.int32)
    for copy in copies:
        copy.wait()
    for patch in range(npatch):
        for at, ref in enumerate(integers):
            numbers = jnp.where(lane == patch * FIELDS + at, ref[patch], numbers)
    shape = (line.shape[0], 1, C)
    line[:, :, npatch * CELLS :] = jnp.broadcast_to(numbers.astype(F32)[None], shape)
    rows = C // P_SIZE
    mine = lax.broadcasted_iota(jnp.int32, (rows, C), 0)
    here = lax.broadcasted_iota(jnp.int32, (rows, C), 1) // P_SIZE == mine
    for patch in range(npatch):
        for at in range(0, P_SIZE, rows):
            part = drawn[patch, at : at + rows, :]
            spread = jnp.concatenate([part] * rows, axis=1)
            flat = jnp.sum(jnp.where(here, spread, 0.0), axis=0, keepdims=True)
            start = patch * CELLS + at * P_SIZE
            line[:, :, start : start + C] = jnp.broadcast_to(flat[None], shape)


def weights_kernel(
    w_a, w_u, b_a, e_a, w_b, b_b, w_o, target,
    weight_a, weight_b, weight_back, ends, target32,
    small_u, small_b, small_e, extra32, field, sems,
):
    taps = 9
    copies = [
        pltpu.make_async_copy(w_b.at[pl.ds(tap * HID, HID)], weight_b.at[:, pl.ds(tap * C, C)], sems.at[tap])
        for tap in range(taps)
    ]
    places = (
        (w_a, weight_a.at[pl.ds(0, taps * C)]),
        (w_u, small_u),
        (b_a, small_b),
        (e_a, small_e),
        (b_b, ends.at[pl.ds(0, 1)]),
        (w_o, ends.at[pl.ds(1, 1)]),
        (target, field),
    )
    smalls = [pltpu.make_async_copy(src, dst, sems.at[taps + at]) for at, (src, dst) in enumerate(places)]
    for copy in smalls + copies:
        copy.start()
    for copy in smalls[1:]:
        copy.wait()
    target32[...] = field[...].astype(F32)
    extra32[...] = jnp.zeros_like(extra32)
    w_u_value, b_a_value, e_a_value = small_u[...], small_b[...], small_e[...]
    extra32[0:taps] = high(w_u_value)
    extra32[taps : 2 * taps] = w_u_value - high(w_u_value)
    extra32[2 * taps : 3 * taps] = high(w_u_value)
    extra32[27:28] = high(b_a_value)
    extra32[28:29] = b_a_value - high(b_a_value)
    extra32[29:30] = high(e_a_value)
    extra32[30:31] = e_a_value - high(e_a_value)
    extra32[31:32] = high(e_a_value)
    weight_a[taps * C :] = extra32[...].astype(BF16)
    for tap, copy in enumerate(copies):
        copy.wait()
        weight_back[tap * C : (tap + 1) * C, :] = weight_b[:, tap * C : (tap + 1) * C].T
    smalls[0].wait()


def train_kernel(
    dp_count,
    npatch,
    table_hbm,
    table,
    features,
    target32_hbm,
    weight_a_hbm,
    weight_b_hbm,
    weight_back_hbm,
    ends_hbm,
    grad_a,
    grad_b,
    send_out,
    loss_out,
    ints,
    chosen,
    blocks,
    target32,
    weight_a,
    weight_b,
    weight_back,
    ends,
    win_a,
    act,
    win_g,
    slope,
    aim,
    tails,
    int_sem,
    weight_sems,
    block_sems,
):
    devices = table.shape[0]
    slots = blocks.shape[0]
    taps = 9
    my_tile, my_dp = lax.axis_index("tile"), lax.axis_index("dp")
    my_core = lax.rem(my_tile * dp_count + my_dp, 2)

    copy_ints = pltpu.make_async_copy(table_hbm.at[:, 0, pl.ds(npatch * CELLS, C)], ints, int_sem)
    copy_ints.start()
    operands = (
        (target32_hbm, target32),
        (ends_hbm, ends),
        (weight_a_hbm, weight_a),
        (weight_b_hbm, weight_b),
        (weight_back_hbm, weight_back),
    )
    copies = [pltpu.make_async_copy(src, dst, weight_sems.at[at]) for at, (src, dst) in enumerate(operands)]
    for copy in copies:
        copy.start()
    copy_ints.wait()

    tile_name = my_tile.astype(F32)

    def choose(device, carry):
        turn, place_at = carry
        for patch in range(npatch):
            owned = ints[device, patch * FIELDS] == tile_name
            mine = jnp.logical_and(owned, turn == my_dp)
            chosen[jnp.where(mine, place_at, slots)] = device * npatch + patch
            place_at = jnp.where(mine, place_at + 1, place_at)
            following = jnp.where(turn == dp_count - 1, 0, turn + 1)
            turn = jnp.where(owned, following, turn)
        return turn, place_at


    def fields(slot):
        patch = chosen[slot]
        device = lax.div(patch, npatch)
        inner = lax.rem(patch, npatch)
        return device, inner

    def block_copy(slot):
        device, inner = fields(slot)
        row = ints[device, inner * FIELDS + 1].astype(jnp.int32)
        column = ints[device, inner * FIELDS + 2].astype(jnp.int32)
        most = (features.shape[1] - SPAN) // 16
        start = jnp.minimum(lax.shift_right_logical(column, 4), most) * 16
        start = pl.multiple_of(start, 16)
        copy = pltpu.make_async_copy(
            features.at[pl.ds(row, P_SIZE), pl.ds(start, SPAN)],
            blocks.at[slot],
            block_sems.at[slot],
        )
        return copy, row, column, column - start

    def start_block(slot, carry):
        block_copy(slot)[0].start()
        return carry

    turn, count = jnp.int32(0), jnp.int32(0)
    stops = [0, devices // 8, devices // 4, devices // 2, devices]
    for begin, end in zip(stops, stops[1:]):
        known = count
        turn, count = lax.fori_loop(begin, end, choose, (turn, known))
        lax.fori_loop(known, count, start_block, 0)

    @pl.when(count == 0)
    def _():
        grad_a[...] = jnp.zeros_like(grad_a)
        grad_b[...] = jnp.zeros_like(grad_b)
        tails[...] = jnp.zeros_like(tails)

    loss_out[...] = jnp.zeros_like(loss_out)
    edge = jnp.zeros((P_SIZE, 3 * C), BF16)
    for part in range(GROUP):
        first, last = part * CELLS, (part + 1) * CELLS - P_SIZE
        win_a[first : first + P_SIZE, : 3 * C] = edge
        win_a[last : last + P_SIZE, 6 * C : 9 * C] = edge
        win_g[last : last + P_SIZE, : 3 * C] = edge
        win_g[first : first + P_SIZE, 6 * C : 9 * C] = edge

    for copy in copies:
        copy.wait()

    cell_col = lax.broadcasted_iota(jnp.int32, (CELLS, C), 0) & (P_SIZE - 1)
    lane = lax.broadcasted_iota(jnp.int32, (CELLS, C), 1)
    lane_tap = lax.rem(lane, taps)
    lane_row, lane_col = lax.div(lane_tap, 3), lax.rem(lane_tap, 3)
    pick_shape = (P_SIZE, P_SIZE, C)
    tile_line = lax.broadcasted_iota(jnp.int32, (P_SIZE * SPAN // 8, 8, C), 1)
    pick_row = lax.broadcasted_iota(jnp.int32, pick_shape, 0) & 7
    pick_col = lax.broadcasted_iota(jnp.int32, pick_shape, 1)
    pick_lane = lax.broadcasted_iota(jnp.int32, pick_shape, 2)
    noise_pick = pick_lane == pick_row * P_SIZE + pick_col
    field_shape = (P_SIZE, P_SIZE, target32.shape[1])
    field_col = lax.broadcasted_iota(jnp.int32, field_shape, 1)
    field_lane = lax.broadcasted_iota(jnp.int32, field_shape, 2)
    loss_row = lax.broadcasted_iota(jnp.int32, loss_out.shape, 0)
    loss_lane = lax.broadcasted_iota(jnp.int32, loss_out.shape, 1)
    log_step = (math.log(SIGMA_HIGH) - math.log(SIGMA_LOW)) / (LEVELS - 1)

    def prepare(part, slot):
        base = part * CELLS
        copy, row, _, offset = block_copy(slot)
        device, inner = fields(slot)
        column = ints[device, inner * FIELDS + 2].astype(jnp.int32)
        level = ints[device, inner * FIELDS + 3]

        tiles = blocks[slot].astype(F32).reshape(P_SIZE * SPAN // 8, 8, C)
        within = offset & 7
        turned = pltpu.roll(tiles, (8 - within) & 7, 1)
        after = jnp.concatenate([turned[1:], turned[:1]], axis=0)
        tiles = jnp.where(tile_line + within < 8, turned, after).reshape(P_SIZE, SPAN // 8, 8, C)
        whole_tiles = lax.shift_right_logical(offset, 3)
        block = jnp.where(
            whole_tiles == 0,
            tiles[:, 0:2],
            jnp.where(whole_tiles == 1, tiles[:, 1:3], tiles[:, 2:4]),
        ).reshape(CELLS, C)
        for shift, value in enumerate(
            (from_previous_column(block, cell_col), block, from_next_column(block, cell_col))
        ):
            value = value.astype(BF16)
            for shift_row in range(3):
                store_window(win_a, base, 3 * shift_row + shift, value)

        log_sigma = math.log(SIGMA_LOW) + jnp.full((1, 1), level) * log_step
        sigma = jnp.exp(log_sigma)
        variance = sigma * sigma + SIGMA_DATA * SIGMA_DATA
        scale_in = 1.0 / jnp.sqrt(variance)
        embed = jnp.log(sigma) / 4.0

        tile_rows = target32.shape[0]
        lines = pltpu.roll(target32[...], lax.rem(tile_rows - row, tile_rows), 0)[:P_SIZE]
        clean = jnp.sum(
            jnp.where(field_lane == column + field_col, lines[:, None, :], 0.0),
            axis=2,
            keepdims=True,
        )
        at = pl.multiple_of(inner * CELLS, C)
        first = table[device, :, pl.ds(at, C)]
        second = table[device, :, pl.ds(pl.multiple_of(at + C, C), C)]
        half = (P_SIZE // 2, P_SIZE, C)
        drawn = jnp.concatenate(
            [jnp.broadcast_to(first[None], half), jnp.broadcast_to(second[None], half)], axis=0
        )
        noise = jnp.sum(jnp.where(noise_pick, drawn, 0.0), axis=2, keepdims=True)
        clean = jnp.broadcast_to(clean, pick_shape).reshape(CELLS, C)
        noise = jnp.broadcast_to(noise, pick_shape).reshape(CELLS, C)
        scaled = scale_in * (clean + sigma * noise)
        aim[base : base + CELLS] = scale_in * (2.0 * sigma * clean - 0.5 * noise)

        rows = jnp.where(
            lane_row == 0,
            from_previous_row(scaled),
            jnp.where(lane_row == 2, from_next_row(scaled), scaled),
        )
        moved = jnp.where(
            lane_col == 0,
            from_previous_column(rows, cell_col),
            jnp.where(lane_col == 2, from_next_column(rows, cell_col), rows),
        )
        moved_high = high(moved)
        value = jnp.where(lane < 2 * taps, moved_high, moved - moved_high)
        embed_high = high(embed)
        rest = jnp.where(
            lane < 29, 1.0, jnp.where(lane < 31, embed_high, embed - embed_high)
        )
        value = jnp.where(lane < 3 * taps, value, jnp.where(lane < 32, rest, 0.0))
        win_a[base : base + CELLS, taps * C :] = value.astype(BF16)

    def work(step, carry):
        slots_at = [step * GROUP + part for part in range(GROUP)]
        real = [slot < count for slot in slots_at]
        used = [jnp.minimum(slot, count - 1) for slot in slots_at]
        for part in range(GROUP):
            @pl.when(real[part])
            def _(part=part):
                block_copy(used[part])[0].wait()

        rows = [slice(part * CELLS, (part + 1) * CELLS) for part in range(GROUP)]

        def first_layer(part):
            return jnp.dot(win_a[rows[part]], weight_a[...], preferred_element_type=F32)

        def activate(part, pre_a):
            gate = sigmoid(pre_a)
            act[rows[part]] = (pre_a * gate).astype(BF16)
            slope[rows[part]] = gate * (1.0 + pre_a * (1.0 - gate))

        def second_layer(part):
            mine = act[rows[part]]
            wide = jnp.dot(mine, weight_b[:, : 8 * C], preferred_element_type=F32)
            last = lax.dot_general(
                weight_back[8 * C :], mine, (((1,), (1,)), ((), ())), preferred_element_type=F32
            )
            return [wide[:, tap * C : (tap + 1) * C] for tap in range(8)] + [last.T]

        def finish(part, product):
            columns = []
            for shift in range(3):
                tap = [product[3 * r + shift] for r in range(3)]
                columns.append(from_previous_row(tap[0]) + tap[1] + from_next_row(tap[2]))
            pre_b = (
                ends[0:1]
                + from_previous_column(columns[0], cell_col)
                + columns[1]
                + from_next_column(columns[2], cell_col)
            )
            gate = sigmoid(pre_b)
            final = jnp.sum(pre_b * gate * ends[1:2], axis=1, keepdims=True)
            residual = final - aim[rows[part]]
            device, inner = fields(used[part])
            weight = jnp.where(real[part], ints[device, inner * FIELDS + 4], 0.0)
            loss = weight * jnp.sum(residual * residual) * (1.0 / (CELLS * C))
            spot = jnp.logical_and(loss_row == device, loss_lane == inner)
            loss_out[...] += jnp.where(spot, loss, 0.0)
            factor = (2.0 / CELLS) * weight * residual
            grad_pre_b = factor * ends[1:2] * (gate * (1.0 + pre_b * (1.0 - gate)))
            base = part * CELLS
            for shift, value in enumerate(
                (
                    from_next_column(grad_pre_b, cell_col),
                    grad_pre_b,
                    from_previous_column(grad_pre_b, cell_col),
                )
            ):
                value = value.astype(BF16)
                for shift_row in range(3):
                    lanes = pl.ds((3 * shift_row + shift) * C, C)
                    if shift_row == 0:
                        win_g[base : base + CELLS - P_SIZE, lanes] = value[P_SIZE:]
                    elif shift_row == 1:
                        win_g[base : base + CELLS, lanes] = value
                    else:
                        win_g[base + P_SIZE : base + CELLS, lanes] = value[: CELLS - P_SIZE]

        def hidden(part):
            return jnp.dot(win_g[rows[part]], weight_back[...], preferred_element_type=F32)

        def turn_back(part, grad_hidden):
            return (grad_hidden * slope[rows[part]]).astype(BF16)

        prepare(0, used[0])
        pre_0 = first_layer(0)
        prepare(1, used[1])
        pre_1 = first_layer(1)
        activate(0, pre_0)
        product_0 = second_layer(0)
        activate(1, pre_1)
        product_1 = second_layer(1)
        finish(0, product_0)
        hidden_0 = hidden(0)
        finish(1, product_1)
        hidden_1 = hidden(1)
        back_0 = turn_back(0, hidden_0)
        started = step > 0
        over_cells = (((0,), (0,)), ((), ()))

        def add(at, grad, rows_of, columns_of):
            wide = columns_of[:, : 8 * C]
            grad[:, : 8 * C] = jnp.where(started, grad[:, : 8 * C], 0.0) + lax.dot_general(
                rows_of, wide, over_cells, preferred_element_type=F32
            )
            last = columns_of[:, 8 * C : 9 * C]
            tails[at] = jnp.where(started, tails[at], 0.0) + lax.dot_general(
                last, rows_of, over_cells, preferred_element_type=F32
            )

        add(1, grad_b, act[...], win_g)
        add(0, grad_a, jnp.concatenate([back_0, turn_back(1, hidden_1)], axis=0), win_a)
        return carry

    lax.fori_loop(0, lax.div(count + GROUP - 1, GROUP), work, 0)
    grad_a[:, 8 * C :] = tails[0].T
    grad_b[:, 8 * C :] = tails[1].T

    chunk = HID // devices
    for pair in range(devices // 2):
        for at, grad in ((0, grad_a), (taps * C, grad_b)):
            even = grad[2 * pair * chunk : (2 * pair + 1) * chunk]
            odd = grad[(2 * pair + 1) * chunk : (2 * pair + 2) * chunk]
            send_out[pair, :, pl.ds(at, taps * C)] = jnp.where(my_core == 0, odd, even).astype(BF16)


def halve_kernel(fan, kept, count, step, *refs):
    keeps, received, outs = refs[:kept], refs[kept : kept + count], refs[kept + count :]
    index = lax.axis_index("tile") * lax.axis_size("dp") + lax.axis_index("dp")
    mine = lax.rem(lax.div(index, step), fan)
    rows = outs[0].shape[0]
    width = outs[0].shape[2] // kept
    for peer in range(fan):
        low = jnp.bitwise_xor(mine, peer)
        for high_part in range(rows):
            at = high_part * fan + low
            for side, keep in enumerate(keeps):
                lanes = slice(side * width, (side + 1) * width)
                total = keep[2 * at + lax.rem(index, 2)] if kept > 1 else keep[at]
                for other in received:
                    total = total + other[at, :, lanes].astype(F32)
                outs[peer][high_part, :, lanes] = total.astype(outs[peer].dtype)


def finish_kernel(npatch, keep, losses, *refs):
    received, (grad, payload) = refs[:-2], refs[-2:]
    total = keep[0]
    for other in received:
        total = total + other[0].astype(F32)
    grad[...] = total
    half = total.shape[1] // 2
    lane = lax.broadcasted_iota(jnp.int32, losses.shape, 1)
    square_a = jnp.sum(total[:, :half] * total[:, :half])
    square_b = jnp.sum(total[:, half:] * total[:, half:])
    value = jnp.where(lane == npatch, square_a, losses[...])
    payload[:, 0, :] = jnp.where(lane == npatch + 1, square_b, value)


def scale_kernel(npatch, entries, grad, payload, losses, upd_a, upd_b):
    total = jnp.sum(payload[:, 0, :], axis=0, keepdims=True)
    lane = lax.broadcasted_iota(jnp.int32, total.shape, 1)
    for patch in range(npatch):
        losses[patch] = jnp.sum(jnp.where(lane == patch, total, 0.0))
    half = grad.shape[1] // 2
    for part, out in enumerate((upd_a, upd_b)):
        square = jnp.sum(jnp.where(lane == npatch + part, total, 0.0), axis=1, keepdims=True)
        out[...] = grad[:, part * half : (part + 1) * half] / jnp.sqrt(square / entries + EPSILON)


def local(
    features,
    target_field,
    owner_tile,
    row_offset,
    column_start,
    noise_level,
    icing_count,
    noise_draw,
    w_a,
    w_u,
    b_a,
    e_a,
    w_b,
    b_b,
    w_o,
):
    tile_count, dp_count = lax.axis_size("tile"), lax.axis_size("dp")
    devices = tile_count * dp_count
    npatch = owner_tile.shape[0]
    slots = max(2, 2 * npatch // tile_count) * devices // dp_count
    chunk = HID // devices
    width = 2 * 9 * C
    in_hbm = pl.BlockSpec(memory_space=pltpu.HBM)
    stay = functools.partial(pltpu.with_memory_space_constraint, memory_space=pltpu.HBM)
    in_vmem = pl.BlockSpec(memory_space=pltpu.VMEM)
    in_smem = pl.BlockSpec(memory_space=pltpu.SMEM)

    def room(mebibytes):
        return pltpu.CompilerParams(vmem_limit_bytes=mebibytes * 1024 * 1024)

    line = pl.pallas_call(
        pack_kernel,
        out_shape=jax.ShapeDtypeStruct((devices, 1, npatch * CELLS + C), F32),
        in_specs=[in_hbm] * 6,
        out_specs=in_vmem,
        scratch_shapes=[
            *[pltpu.SMEM((npatch,), jnp.int32)] * 5,
            pltpu.VMEM(noise_draw.shape, F32),
            pltpu.SemaphoreType.DMA((6,)),
        ],
        compiler_params=room(4),
        name="pack",
    )(
        *map(stay, (owner_tile.reshape(-1), row_offset, column_start, noise_level, icing_count, noise_draw))
    )
    table = lax.all_to_all(line, AXES, split_axis=0, concat_axis=0, tiled=True)

    weights = pl.pallas_call(
        weights_kernel,
        out_shape=(
            pltpu.HBM((10 * C, HID), BF16),
            pltpu.HBM((HID, 9 * C), BF16),
            pltpu.HBM((9 * C, HID), BF16),
            pltpu.HBM((2, C), F32),
            pltpu.HBM(target_field.shape, F32),
        ),
        in_specs=[in_hbm] * 8,
        out_specs=(in_vmem,) * 5,
        scratch_shapes=[
            pltpu.VMEM((9, HID), F32),
            pltpu.VMEM((1, HID), F32),
            pltpu.VMEM((1, HID), F32),
            pltpu.VMEM((C, HID), F32),
            pltpu.VMEM(target_field.shape, BF16),
            pltpu.SemaphoreType.DMA((16,)),
        ],
        compiler_params=room(8),
        name="weights",
    )(
        stay(w_a),
        stay(w_u),
        stay(b_a.reshape(1, -1)),
        stay(e_a.reshape(1, -1)),
        stay(w_b),
        stay(b_b.reshape(1, -1)),
        stay(w_o.reshape(1, -1)),
        stay(target_field),
    )
    weight_a, weight_b, weight_back, ends, target32 = weights

    grad_a, grad_b, send, losses = pl.pallas_call(
        functools.partial(train_kernel, dp_count, npatch),
        out_shape=(
            pltpu.VMEM((HID, 9 * C), F32),
            pltpu.VMEM((HID, 9 * C), F32),
            pltpu.VMEM((devices // 2, chunk, width), BF16),
            pltpu.VMEM((devices, C), F32),
        ),
        in_specs=[in_hbm, in_vmem] + [in_hbm] * 6,
        out_specs=(in_vmem,) * 4,
        scratch_shapes=[
            pltpu.SMEM((devices, C), F32),
            pltpu.SMEM((slots + 1,), jnp.int32),
            pltpu.VMEM((slots, P_SIZE, SPAN, C), BF16),
            pltpu.VMEM(target_field.shape, F32),
            pltpu.VMEM((10 * C, HID), BF16),
            pltpu.VMEM((HID, 9 * C), BF16),
            pltpu.VMEM((9 * C, HID), BF16),
            pltpu.VMEM((2, C), F32),
            pltpu.VMEM((GROUP * CELLS, 10 * C), BF16),
            pltpu.VMEM((GROUP * CELLS, HID), BF16),
            pltpu.VMEM((GROUP * CELLS, 9 * C), BF16),
            pltpu.VMEM((GROUP * CELLS, HID), F32),
            pltpu.VMEM((GROUP * CELLS, C), F32),
            pltpu.VMEM((2, C, HID), F32),
            pltpu.SemaphoreType.DMA,
            pltpu.SemaphoreType.DMA((5,)),
            pltpu.SemaphoreType.DMA((slots,)),
        ],
        compiler_params=room(32),
        name="train",
    )(table, table, *map(stay, (features, target32, weight_a, weight_b, weight_back, ends)))

    def exchange(array, distance):
        return lax.ppermute(array, AXES, [(i, i ^ distance) for i in range(devices)])

    received = [exchange(send, 1)]
    keeps = [grad.reshape(devices, chunk, 9 * C) for grad in (grad_a, grad_b)]
    rows = devices // 2
    step = 2
    while step < devices:
        fan = min(8, devices // step)
        rows //= fan
        part = (rows, chunk, width)
        outs = pl.pallas_call(
            functools.partial(halve_kernel, fan, len(keeps), len(received), step),
            out_shape=(
                pltpu.VMEM(part, F32),
                *[pltpu.VMEM(part, BF16) for _ in range(fan - 1)],
            ),
            in_specs=[in_vmem] * (len(keeps) + len(received)),
            out_specs=(in_vmem,) * fan,
            compiler_params=room(16),
            name=f"halve_{step}",
        )(*keeps, *received)
        keeps = outs[:1]
        order = sorted(range(1, fan), key=lambda peer: ((0, 0, 2, 1)[peer.bit_count()], peer))
        received = [exchange(outs[peer], peer * step) for peer in order]
        step *= fan

    grad, payload = pl.pallas_call(
        functools.partial(finish_kernel, npatch),
        out_shape=(
            pltpu.VMEM((chunk, width), F32),
            pltpu.VMEM((devices, 1, C), F32),
        ),
        in_specs=[in_vmem] * (2 + len(received)),
        out_specs=(in_vmem, in_vmem),
        compiler_params=room(4),
        name="finish",
    )(*keeps, losses, *received)
    payload = lax.all_to_all(payload, AXES, split_axis=0, concat_axis=0, tiled=True)
    out = jax.ShapeDtypeStruct((chunk, width // 2), F32)
    sums, upd_a, upd_b = pl.pallas_call(
        functools.partial(scale_kernel, npatch, HID * 9 * C),
        out_shape=(jax.ShapeDtypeStruct((npatch,), F32), out, out),
        in_specs=[in_vmem, in_vmem],
        out_specs=(in_smem, in_vmem, in_vmem),
        compiler_params=room(4),
        name="scale",
    )(grad, payload)
    return sums, upd_a, upd_b


def solution(mesh):
    both = P(AXES)
    return jax.shard_map(
        local,
        mesh=mesh,
        in_specs=(
            P("tile", None, None),
            P("tile", None),
            P(AXES, None),
            both,
            both,
            both,
            both,
            P(AXES, None, None),
            P(),
            P(),
            P(),
            P(),
            P(),
            P(),
            P(),
        ),
        out_specs=(both, P(AXES, None), P(AXES, None)),
        check_vma=False,
    )
```
